256 devices in a mesh: mem: 64 (over z, y, core), rep: 4 (over x).
Axes of the slice: x: 4, y: 4, z: 8, core: 2. Of those that a mesh axis runs over, the one named last changes fastest.
Arguments:
- memory: bfloat16 [4, 131072, 512], P('rep', 'mem'), may hold values from -6 to 6
- endpoint_owner: int32 [4, 2, 16384, 2], P('rep', None, 'mem'), may hold values from 0 to 63, all different within a row; in each aligned block of 256 rows (0 to 255, 256 to 511, ..., all dimensions but the last counted through in order) at most 16 rows name the same one
- endpoint_row: int32 [4, 2, 16384, 2], P('rep', None, 'mem'), may hold values from 0 to 2047
- event_time: int32 [4, 2, 16384], P('rep', None, 'mem'), may hold values from 1024 to 2047
- neighbour_time: int32 [4, 2, 16384], P('rep', None, 'mem'), may hold values from 0 to 1023
- neighbour_feat: bfloat16 [4, 2, 16384, 512], P('rep', None, 'mem'), may hold values from -6 to 6
- neighbour_index: int32 [4, 2, 16384, 128], P('rep', None, 'mem'), may hold values from 0 to 255
- valid_length: int32 [4, 2, 16384], P('rep', None, 'mem'), may hold values from 1 to 128, as said below
- decay_rate: float32 [8], replicated, may hold values from 0.02 to 2
- w_query: bfloat16 [512, 512], replicated, may hold values from -0.25 to 0.25
- w_keyval: bfloat16 [512, 1024], replicated, may hold values from -0.25 to 0.25
- w_out: bfloat16 [512, 512], replicated, may hold values from -0.25 to 0.25
- gru_input: bfloat16 [512, 1536], replicated, may hold values from -0.25 to 0.25
- gru_hidden: bfloat16 [512, 1536], replicated, may hold values from -0.25 to 0.25
- cotangent: bfloat16 [4, 2, 16384, 512], P('rep', None, 'mem'), may hold values from -6 to 6
Outputs:
- new_memory: bfloat16 [4, 131072, 512], P('rep', 'mem')
- embeddings: bfloat16 [4, 2, 16384, 512], P('rep', None, 'mem')
- grad_query: float32 [512, 512], P('mem')
- grad_keyval: float32 [512, 1024], P('mem')
- grad_out: float32 [512, 512], P('mem')
The draws below stay inside these ranges and needn't reach their ends.
Inputs may be any that keep to these rules, and one draw needn't show every extreme that they name: `endpoint_owner`: within the events of one device in one batch (aligned blocks of 256 events), no shard is named more than 16 times, some shard exactly 16 times; the two endpoints of an event lie on different shards. `neighbour_index`: an index into the 256 neighbour rows of the event's block; indices may repeat and each listed entry counts. `valid_length`: the first event of every block has 128 listed neighbours.
All inputs are finite; a program needn't handle non-finite values.
Results may differ from the reference program's by a relative error of at most 0.017.
Values may be sent and summed in bfloat16 or wider, within the bound.
A program may use at most 128 MiB of HBM per device.

```python
import math
import jax
import jax.numpy as jnp
import numpy as np
from jax import lax

D = 512
HEADS = 8
NBRS = 128
BATCHES = 2
EV_DEV = 256
NODE_DEV = 2048
NBR_DEV = 256
OWNERS = 64
CAP = 16
EVENTS = 16384
NODES = 131072
NBR_ROWS = 16384
N_REP = 4


def draw_valid_length(key, part):
    key = jax.random.fold_in(key, 7)
    lengths = jax.random.randint(key, (N_REP, BATCHES, EVENTS), 1, NBRS + 1, dtype=jnp.int32)
    return lengths.at[:, :, ::EV_DEV].set(NBRS)


def touch_ends(result, stream_key, low, largest):
    longest = result.shape.index(max(result.shape))
    spots = []
    for shift in (0, 1):
        where = [jax.random.randint(jax.random.fold_in(stream_key, axis), (), 0, length) for axis, length in enumerate(result.shape)]
        where[longest] = (where[longest] + shift) % result.shape[longest]
        spots.append(tuple(where))
    return result.at[spots[0]].set(low).at[spots[1]].set(largest)


def level_of(stream_key, extent, shards, least, top_value):
    level = 1.0
    for position, shards_of in shards:
        draws = jax.random.uniform(jax.random.fold_in(jax.random.fold_in(stream_key, 6), position), (shards_of,), jnp.float32, least / len(shards), top_value / len(shards))
        level = level * jnp.repeat(jnp.exp(draws), extent[position] // shards_of).reshape((-1,) + (1,) * (len(extent) - 1 - position))
    return level


def routed_block(key, own, number, rows, number_of, top, most, skew):
    order = jax.random.permutation(key, number_of)
    heavy_load, usual = load_shares(number_of, rows * top, most, skew, True), load_shares(number_of, rows * top, most, skew, False)
    places = jnp.arange(number_of)

    def named(sizes, offset_by):
        used = int((sizes > 0).sum())
        fixed = max(1, used // 4)
        moved = fixed + (places - fixed + offset_by * (used - fixed)) % max(1, number_of - fixed)
        return jnp.zeros((number_of,), jnp.int32).at[order[jnp.where(places < fixed, places, moved)]].set(jnp.asarray(sizes, jnp.int32))

    sizes = jnp.where(number % 4 == 0, named(heavy_load, number // 4), named(usual, number - number // 4 - 1))
    mixed = jax.random.permutation(jax.random.fold_in(own, 3), number_of)
    source_of, sink = mixed[0:number_of // 2 * 2:2], mixed[1:number_of // 2 * 2:2]
    room = jnp.minimum(sizes[source_of] - 1, most - sizes[sink]) // 2
    room = jnp.where((source_of == order[0]) | (sink == order[0]) | (sizes[sink] == 0), 0, jnp.maximum(room, 0))
    moved = jax.random.randint(jax.random.fold_in(own, 4), (number_of // 2,), 0, 1 << 20) % (room + 1)
    sizes = sizes.at[source_of].add(-moved).at[sink].add(moved)
    items = jnp.searchsorted(jnp.cumsum(sizes), jnp.arange(rows * top), side="right").astype(jnp.int32)
    grid = items.reshape(top, rows).T
    grid = grid[jax.random.permutation(jax.random.fold_in(own, 1), rows)]
    offset_by = jax.random.randint(jax.random.fold_in(own, 2), (rows, 1), 0, top)
    return jnp.take_along_axis(grid, (jnp.arange(top)[None, :] + offset_by) % top, axis=1)


def load_shares(number_of, total, reach, skew, full):
    weights = [(1 << 20) // math.isqrt(standing ** skew) + 1 for standing in range(1, number_of + 1)]
    largest = reach if full else min(reach, max(-(-total // number_of), total * weights[0] // sum(weights)))
    least = 1 if total - largest >= number_of - 1 else 0
    holding, surplus = [largest] + [least] * (number_of - 1), total - largest - least * (number_of - 1)
    while surplus > 0:
        free = [i for i in range(1, number_of) if holding[i] < largest] or [i for i in range(1, number_of) if holding[i] < reach]
        mass, left = sum([weights[i] for i in free]), surplus
        for i in free:
            more = min(reach - holding[i], max(1, left * weights[i] // mass), surplus)
            holding[i] = holding[i] + more
            surplus = surplus - more
    return np.array(holding)


def scatter_about(stream_key, dims, scale, most, shards=(), kind=jnp.bfloat16):
    drawn = jax.random.normal(stream_key, dims, jnp.float32) * scale
    if len(shards) > 0:
        drawn = level_of(stream_key, dims, shards, -0.22, 0.18) * drawn
    return jnp.clip(drawn, min=-most, max=most).astype(kind)


def setup_inputs(seed: int = 0) -> dict:
    arg_keys = jax.random.split(jax.random.key(seed), 16)
    memory = scatter_about(arg_keys[0], (N_REP, NODES, D), 1.0, 6.0, ((0, 4), (1, 64)))
    endpoint_owner_keys = jax.random.split(jax.random.fold_in(arg_keys[1], 1), N_REP * BATCHES * EVENTS // EV_DEV)
    endpoint_owner_turns = jax.random.permutation(jax.random.fold_in(arg_keys[1], 3), N_REP * BATCHES * EVENTS // EV_DEV)
    endpoint_owner = jax.vmap(lambda own, number: routed_block(jax.random.fold_in(arg_keys[1], 2), own, number, EV_DEV, OWNERS, 2, CAP, 2))(endpoint_owner_keys, endpoint_owner_turns).reshape((N_REP, BATCHES, EVENTS, 2))
    endpoint_row = touch_ends(jax.random.randint(arg_keys[2], (N_REP, BATCHES, EVENTS, 2), 0, NODE_DEV), jax.random.fold_in(arg_keys[2], 1), 0, NODE_DEV - 1).astype(jnp.int32)
    event_time = touch_ends(jax.random.randint(arg_keys[3], (N_REP, BATCHES, EVENTS), 1024, 2048), jax.random.fold_in(arg_keys[3], 1), 1024, 2047).astype(jnp.int32)
    neighbour_time = touch_ends(jax.random.randint(arg_keys[4], (N_REP, BATCHES, NBR_ROWS), 0, 1024), jax.random.fold_in(arg_keys[4], 1), 0, 1023).astype(jnp.int32)
    neighbour_feat = scatter_about(arg_keys[5], (N_REP, BATCHES, NBR_ROWS, D), 1.0, 6.0, ((0, 4), (2, 64)))
    neighbour_index = touch_ends(jax.random.randint(arg_keys[6], (N_REP, BATCHES, EVENTS, NBRS), 0, NBR_DEV), jax.random.fold_in(arg_keys[6], 1), 0, NBR_DEV - 1).astype(jnp.int32)
    valid_length = draw_valid_length(jax.random.fold_in(arg_keys[15], 71), 0)
    decay_rate = jnp.clip(jnp.exp(jax.random.uniform(arg_keys[8], (HEADS,), jnp.float32, math.log(0.02), math.log(2.0))), 0.02, 2.0)
    w_query = scatter_about(arg_keys[9], (D, D), D ** -0.5, 0.25)
    w_keyval = scatter_about(arg_keys[10], (D, 2 * D), D ** -0.5, 0.25)
    w_out = scatter_about(arg_keys[11], (D, D), D ** -0.5, 0.25)
    gru_input = scatter_about(arg_keys[12], (D, 3 * D), D ** -0.5, 0.25)
    gru_hidden = scatter_about(arg_keys[13], (D, 3 * D), D ** -0.5, 0.25)
    cotangent = scatter_about(arg_keys[14], (N_REP, BATCHES, EVENTS, D), 1.0, 6.0, ((0, 4), (2, 64)))
    return {"memory": memory, "endpoint_owner": endpoint_owner, "endpoint_row": endpoint_row, "event_time": event_time, "neighbour_time": neighbour_time, "neighbour_feat": neighbour_feat, "neighbour_index": neighbour_index, "valid_length": valid_length, "decay_rate": decay_rate, "w_query": w_query, "w_keyval": w_keyval, "w_out": w_out, "gru_input": gru_input, "gru_hidden": gru_hidden, "cotangent": cotangent}


def attend(w_query, w_keyval, w_out, source, features, neighbour_index, valid_length, event_time, neighbour_time, decay_rate):
    events, width = source.shape
    head_count = decay_rate.shape[0]
    head_width = width // head_count
    rows_total = features.shape[0]
    listed = (jnp.arange(neighbour_index.shape[1], dtype=jnp.int32)[None, :] < valid_length[:, None]).astype(jnp.float32)
    multiplicity = jnp.zeros((events, rows_total), jnp.float32).at[jnp.arange(events, dtype=jnp.int32)[:, None], neighbour_index].add(listed)
    query_rows = jnp.dot(source, w_query, preferred_element_type=jnp.float32).astype(jnp.bfloat16)
    query_rows = query_rows.reshape(events, head_count, head_width)
    keyval = jnp.dot(features, w_keyval, preferred_element_type=jnp.float32).astype(jnp.bfloat16)
    key_rows = keyval[:, :width].reshape(rows_total, head_count, head_width)
    value_rows = keyval[:, width:].reshape(rows_total, head_count, head_width)
    scores = jnp.einsum('ehd,rhd->her', query_rows.astype(jnp.float32), key_rows.astype(jnp.float32)) / math.sqrt(head_width)
    elapsed = jnp.log1p((event_time[:, None] - neighbour_time[None, :]).astype(jnp.float32))
    logits = scores - decay_rate[:, None, None] * elapsed[None]
    is_live = multiplicity[None] > 0
    row_max = lax.stop_gradient(lax.optimization_barrier(jnp.max(jnp.where(is_live, logits, -1e+30), axis=-1, keepdims=True)))
    weighted = multiplicity[None] * jnp.exp(jnp.where(is_live, logits - row_max, -1e+30))
    weights = (weighted / lax.optimization_barrier(jnp.sum(weighted, axis=-1, keepdims=True))).astype(jnp.bfloat16)
    attended = jnp.einsum('her,rhd->ehd', weights.astype(jnp.float32), value_rows.astype(jnp.float32))
    attended = attended.reshape(events, width).astype(jnp.bfloat16)
    return (source.astype(jnp.float32) + jnp.dot(attended, w_out, preferred_element_type=jnp.float32)).astype(jnp.bfloat16)

def gru_step(state_rows, other_rows, gru_input, gru_hidden):
    half = state_rows.shape[1]
    input_gates = jnp.dot(other_rows, gru_input, preferred_element_type=jnp.float32)
    hidden_gates = jnp.dot(state_rows, gru_hidden, preferred_element_type=jnp.float32)
    reset_gate = jax.nn.sigmoid(input_gates[:, :half] + hidden_gates[:, :half])
    update_gate = jax.nn.sigmoid(input_gates[:, half:2 * half] + hidden_gates[:, half:2 * half])
    candidate = jnp.tanh(input_gates[:, 2 * half:] + reset_gate * hidden_gates[:, 2 * half:])
    return ((1.0 - update_gate) * candidate + update_gate * state_rows.astype(jnp.float32)).astype(jnp.bfloat16)

def apply_updates(memory_rows, node_ids, updated, node_total):
    row_sums = jax.ops.segment_sum(updated.astype(jnp.float32), node_ids, node_total)
    row_counts = jax.ops.segment_sum(jnp.ones(node_ids.shape, jnp.float32), node_ids, node_total)
    averaged = row_sums / jnp.maximum(row_counts, 1.0)[:, None]
    return jnp.where(row_counts[:, None] > 0, averaged, memory_rows.astype(jnp.float32)).astype(jnp.bfloat16)

def reference(memory, endpoint_owner, endpoint_row, event_time, neighbour_time, neighbour_feat, neighbour_index, valid_length, decay_rate, w_query, w_keyval, w_out, gru_input, gru_hidden, cotangent):
    totals = (jnp.zeros((D, D), jnp.float32), jnp.zeros((D, 2 * D), jnp.float32), jnp.zeros((D, D), jnp.float32))
    new_streams = []
    all_embeddings = []
    for replica in range(N_REP):
        memory_rows = memory[replica]
        stream_embeddings = []
        for batch_index in range(BATCHES):
            node_ids = (endpoint_owner[replica, batch_index] * NODE_DEV + endpoint_row[replica, batch_index]).reshape(-1)
            paired = jnp.take(memory_rows, node_ids, axis=0).reshape(EVENTS, 2, D)
            source = paired[:, 0]
            block_data = (source.reshape(OWNERS, EV_DEV, D), neighbour_feat[replica, batch_index].reshape(OWNERS, NBR_DEV, D), neighbour_index[replica, batch_index].reshape(OWNERS, EV_DEV, NBRS), valid_length[replica, batch_index].reshape(OWNERS, EV_DEV), event_time[replica, batch_index].reshape(OWNERS, EV_DEV), neighbour_time[replica, batch_index].reshape(OWNERS, NBR_DEV), cotangent[replica, batch_index].reshape(OWNERS, EV_DEV, D))

            def scan_step(running, block_item):
                block_source, block_feat, block_index, block_length, block_time, block_ntime, block_cot = block_item

                def forward(query_weight, keyval_weight, out_weight):
                    return attend(query_weight, keyval_weight, out_weight, block_source, block_feat, block_index, block_length, block_time, block_ntime, decay_rate)
                embedding, pullback = jax.vjp(forward, w_query, w_keyval, w_out)
                gradients = pullback(block_cot)
                running = tuple((total + grad.astype(jnp.float32) for total, grad in zip(running, gradients)))
                return (running, embedding)
            totals, block_embeddings = lax.scan(scan_step, totals, block_data)
            stream_embeddings.append(block_embeddings.reshape(EVENTS, D))
            endpoint_rows = paired.reshape(2 * EVENTS, D)
            partner = paired[:, ::-1].reshape(2 * EVENTS, D)
            updated = gru_step(endpoint_rows, partner, gru_input, gru_hidden)
            memory_rows = apply_updates(memory_rows, node_ids, updated, NODES)
        new_streams.append(memory_rows)
        all_embeddings.append(jnp.stack(stream_embeddings))
    return (jnp.stack(new_streams), jnp.stack(all_embeddings), totals[0], totals[1], totals[2])
```

```python
import functools
import math

import jax
import jax.numpy as jnp
from jax import lax
from jax.experimental import pallas as pl
from jax.experimental.pallas import tpu as pltpu
from jax.sharding import PartitionSpec as P

MESH = pl.DeviceIdType.MESH
BF = jnp.bfloat16
F32 = jnp.float32
I32 = jnp.int32
CAP = 16
PLANE = 8
GROUP = CAP * PLANE
HEADS = 8
NY = 4


def nn(a, b):
    return lax.dot_general(a, b, (((1,), (0,)), ((), ())), preferred_element_type=F32)


def nt(a, b):
    return lax.dot_general(a, b, (((1,), (1,)), ((), ())), preferred_element_type=F32)


def sigmoid(a):
    return 0.5 * jnp.tanh(0.5 * a) + 0.5


def iota(shape, axis):
    return lax.broadcasted_iota(I32, shape, axis)


def one_hot(mask):
    return jnp.where(mask, 1.0, 0.0).astype(BF)


def window(
    nx,
    owner_ref,
    row_ref,
    et_ref,
    nt_ref,
    vl_ref,
    decay_ref,
    nidx_ref,
    mem_ref,
    feat_ref,
    cot_ref,
    wq_ref,
    wkv_ref,
    wo_ref,
    gi_ref,
    gh_ref,
    newmem_ref,
    emb_ref,
    gq_ref,
    gkv_ref,
    go_ref,
    ids_out,
    ids_in,
    served,
    answered,
    outgoing,
    arrived,
    mem1,
    slot_ref,
    lane_ref,
    col_ref,
    pick_ref,
    rows_ref,
    upd_ref,
    idx_ref,
    mult_ref,
    elapsed_ref,
    kv_ref,
    kvt_ref,
    q_ref,
    datt_ref,
    att_ref,
    dq_ref,
    dkv_ref,
    ga_ref,
    gb_ref,
    h1,
    r1,
    h2,
    r2,
    h3,
    r3,
    h4,
    r4,
    fin,
    send_sem,
    recv_sem,
):
    n = ids_in.shape[0]
    nz = n // PLANE
    nodes, width = mem_ref.shape
    events = et_ref.shape[1]
    nbrs = nt_ref.shape[1]
    ends = 2 * events
    slots = n * CAP
    me = lax.axis_index("mem")
    x = lax.axis_index("rep")
    z = me // PLANE
    yc = me % PLANE
    y = yc // 2
    c = yc % 2

    barrier = pltpu.get_barrier_semaphore()

    @pl.loop(1, n)
    def _(k):
        pl.semaphore_signal(barrier, inc=1, device_id={"mem": (me + k) % n}, device_id_type=MESH)

    for k in range(1, nx):
        pl.semaphore_signal(barrier, inc=1, device_id={"rep": (x + k) % nx}, device_id_type=MESH)

    def group_at(i):
        h = (i + 1) // 2
        return nz // 2 + h * (1 - 2 * (i % 2))

    def start_group(src, dst, g, length, sem):
        @pl.loop(0, PLANE)
        def _(j):
            @pl.when(g * PLANE + j > 0)
            def _():
                q = g * PLANE + (j + yc) % PLANE
                other = (q + z * PLANE) % n
                mine = (me + n - (other // PLANE) * PLANE) % n
                pltpu.make_async_remote_copy(
                    src_ref=src.at[pl.ds(pl.multiple_of(q * length, length), length)],
                    dst_ref=dst.at[pl.ds(pl.multiple_of(mine * length, length), length)],
                    send_sem=send_sem.at[sem],
                    recv_sem=recv_sem.at[sem],
                    device_id={"mem": other},
                    device_id_type=MESH,
                ).start()

    def own_block(src, dst):
        here = pl.ds(pl.multiple_of(yc * CAP, CAP), CAP)
        dst[here, :] = src[here, :]

    def wait_sent(view, sem):
        pltpu.make_async_copy(view, view, send_sem.at[sem]).wait()

    def wait_got(view, sem):
        pltpu.make_async_copy(view, view, recv_sem.at[sem]).wait()

    before = one_hot(iota((ends, ends), 0) < iota((ends, ends), 1))
    for b in range(2):
        own = owner_ref[b : b + 1, :] - z * PLANE
        own = jnp.where(own < 0, own + n, own)
        marks = jnp.where(iota((n, ends), 0) == own, 1.0, 0.0)
        marks_bf = marks.astype(BF)
        rank = jnp.sum(nn(marks_bf, before) * marks, axis=0, keepdims=True).astype(I32)
        slot_ref[b : b + 1, :] = own * CAP + rank
        wanted = row_ref[b : b + 1, :] + 1
        here = (iota((128, ends), 0) % CAP) == rank
        high = jnp.where(here, (wanted // 64).astype(F32), 0.0).astype(BF)
        low = jnp.where(here, (wanted % 64).astype(F32), 0.0).astype(BF)
        found = nt(marks_bf, high) * 64.0 + nt(marks_bf, low)
        ids_out[:, :, b * 128 : (b + 1) * 128] = (found.astype(I32) - 1).reshape(n, 1, 128)

    pl.semaphore_wait(barrier, n - 1 + nx - 1)

    @pl.loop(0, nz)
    def _(i):
        start_group(ids_out, ids_in, group_at(i), 1, 0)

    ids_in[pl.ds(yc, 1)] = ids_out[pl.ds(yc, 1)]
    wait_got(ids_in.at[pl.ds(0, n - 1)], 0)
    wait_sent(ids_out.at[pl.ds(0, n - 1)], 0)

    for b in range(2):
        seen = ids_in[:, :, b * 128 : (b + 1) * 128].reshape(n, 128).astype(F32)
        mine = (iota((n, 128), 0) % PLANE) == (iota((n, 128), 1) // CAP)
        packed = jnp.sum(jnp.where(mine, seen, 0.0).reshape(nz, PLANE, 128), axis=1)
        for g in range(nz):
            row = packed[g : g + 1, :]
            lane_ref[b : b + 1, g * GROUP : (g + 1) * GROUP] = row.astype(I32)
            col_ref[b, g * GROUP : (g + 1) * GROUP, :] = jnp.broadcast_to(row, (128, 128)).T.astype(I32)

    def serve(b, source):
        per = 2 if nz % 2 == 0 else 1

        @pl.loop(0, nz // per)
        def _(i):
            groups = [group_at(per * i + t) for t in range(per)]
            places = [pl.ds(pl.multiple_of(g * GROUP, GROUP), GROUP) for g in groups]
            wanted = jnp.concatenate([col_ref[b, p, 0:1] for p in places], axis=0)
            pick = one_hot(wanted == iota((per * GROUP, nodes), 1))
            got = nn(pick, source[...]).astype(BF)
            for t in range(per):
                served[b, places[t], :] = got[t * GROUP : (t + 1) * GROUP]
            for t in range(per):
                start_group(served.at[b], answered.at[b], groups[t], CAP, 1 + b)

        own_block(served.at[b], answered.at[b])

    def prepare(b):
        kv = nn(feat_ref[b], wkv_ref[...]).astype(BF)
        kv_ref[b] = kv
        kvt_ref[b] = kv.T
        slot_col = jnp.broadcast_to(slot_ref[b : b + 1, :].astype(F32), (128, ends)).T.astype(I32)
        pick_ref[b] = one_hot(slot_col[:, 0:1] == iota((ends, slots), 1))
        since = jnp.broadcast_to(nt_ref[b : b + 1, :].astype(F32), (128, nbrs)).T
        elapsed_ref[b] = jnp.log(1.0 + (et_ref[b : b + 1, :].astype(F32) - since[:, 0:1]))
        listed = nidx_ref[b].astype(F32).T
        count = listed.shape[0]
        idx_ref[...] = jnp.where(iota((count, events), 0) < vl_ref[b : b + 1, :], listed, -1.0).astype(I32)
        step = min(64, nbrs)

        @pl.loop(0, nbrs // step)
        def _(k):
            place = iota((step, events), 0) + k * step

            def add(j, total):
                rows = idx_ref[pl.ds(pl.multiple_of(j * 8, 8), 8), :]
                for t in range(8):
                    total = total + jnp.where(place == rows[t : t + 1, :], 1.0, 0.0)
                return total

            mult_ref[b, pl.ds(pl.multiple_of(k * step, step), step), :] = lax.fori_loop(
                0, count // 8, add, jnp.zeros((step, events), F32)
            )

    def fetch(b):
        wait_got(answered.at[b, pl.ds(0, slots - CAP)], 1 + b)
        got = nn(pick_ref[b], answered[b]).astype(BF)
        rows_ref[b, 0] = got[:events]
        rows_ref[b, 1] = got[events:]

    def update(b):
        @pl.loop(0, 2)
        def _(k):
            state = rows_ref[b, k]
            partner = rows_ref[b, 1 - k]
            gates = nn(partner, gi_ref[:, : 2 * width]) + nn(state, gh_ref[:, : 2 * width])
            reset = sigmoid(gates[:, :width])
            keep = sigmoid(gates[:, width:])
            candidate = jnp.tanh(
                nn(partner, gi_ref[:, 2 * width :]) + reset * nn(state, gh_ref[:, 2 * width :])
            )
            upd_ref[pl.ds(pl.multiple_of(k * events, events), events), :] = (
                candidate + keep * (state.astype(F32) - candidate)
            ).astype(BF)

        per = 2 if nz % 2 == 0 else 1

        @pl.loop(0, nz // per)
        def _(i):
            groups = [group_at(per * i + t) for t in range(per)]
            place = jnp.concatenate([iota((GROUP, ends), 0) + g * GROUP for g in groups], axis=0)
            got = nn(one_hot(place == slot_ref[b : b + 1, :]), upd_ref[...]).astype(BF)
            for t in range(per):
                at = pl.ds(pl.multiple_of(groups[t] * GROUP, GROUP), GROUP)
                outgoing[b, at, :] = got[t * GROUP : (t + 1) * GROUP]
            for t in range(per):
                start_group(outgoing.at[b], arrived.at[b], groups[t], CAP, 3 + b)

        own_block(outgoing.at[b], arrived.at[b])

    def apply(b, source, target):
        wait_got(arrived.at[b, pl.ds(0, slots - CAP)], 3 + b)
        step = min(512, nodes)

        @pl.loop(0, nodes // step)
        def _(k):
            at = pl.ds(pl.multiple_of(k * step, step), step)
            marks = jnp.where(iota((step, slots), 0) + k * step == lane_ref[b : b + 1, :], 1.0, 0.0)
            counts = jnp.sum(marks, axis=1, keepdims=True)
            sums = nn(marks.astype(BF), arrived[b])
            mean = sums * (1.0 / jnp.maximum(counts, 1.0))
            target[at, :] = jnp.where(counts > 0, mean, source[at, :].astype(F32)).astype(BF)

    def attend(b):
        source = rows_ref[b, 0]
        cot = cot_ref[b]
        q_ref[...] = nn(source, wq_ref[...]).astype(BF)
        datt_ref[...] = nt(cot, wo_ref[...]).astype(BF)
        scale = 1.0 / math.sqrt(width // HEADS)
        half_width = width // HEADS

        @pl.loop(0, HEADS // 2)
        def _(pair):
            cols = pl.ds(pl.multiple_of(pair * 2 * half_width, 2 * half_width), 2 * half_width)
            vcols = pl.ds(pl.multiple_of(width + pair * 2 * half_width, 2 * half_width), 2 * half_width)
            keys = kv_ref[b, :, cols]
            values = kv_ref[b, :, vcols]
            q_pair = q_ref[:, cols]
            d_pair = datt_ref[:, cols]
            dk = jnp.zeros((nbrs, 2 * half_width), F32)
            dv = jnp.zeros((nbrs, 2 * half_width), F32)
            for half in range(2):
                head = 2 * pair + half
                lanes = one_hot(iota((1, 2 * half_width), 1) // half_width == half)
                q = q_pair * lanes
                d = d_pair * lanes
                mult = mult_ref[b]
                live = mult > 0
                logits = nt(keys, q) * scale - decay_ref[head] * elapsed_ref[b]
                top = jnp.max(jnp.where(live, logits, -1e30), axis=0, keepdims=True)
                weighted = mult * jnp.exp(jnp.where(live, logits - top, -1e30))
                weights = weighted * (1.0 / jnp.sum(weighted, axis=0, keepdims=True))
                w = weights.astype(BF)
                at = pl.ds(pl.multiple_of(head * half_width, half_width), half_width)
                vat = pl.ds(pl.multiple_of(width + head * half_width, half_width), half_width)
                att_ref[at, :] = nn(kvt_ref[b, vat, :], w).astype(BF)
                dw = nt(values, d)
                inner = jnp.sum(dw * weights, axis=0, keepdims=True)
                dl = (weights * (dw - inner) * scale).astype(BF)
                dq_ref[at, :] = nn(kvt_ref[b, at, :], dl).astype(BF)
                dv = dv + nn(w, d)
                dk = dk + nn(dl, q)
            dkv_ref[:, cols] = dk.astype(BF)
            dkv_ref[:, vcols] = dv.astype(BF)

        emb_ref[b] = (source.astype(F32) + nn(att_ref[...].T, wo_ref[...])).astype(BF)
        go = nn(att_ref[...], cot)
        gq = nn(source.T, dq_ref[...].T)
        gkv = nn(feat_ref[b].T, dkv_ref[...])
        if b == 0:
            ga_ref[:, :width] = gq
            ga_ref[:, width:] = go
            gb_ref[...] = gkv
        else:
            ga_ref[:, :width] += gq
            ga_ref[:, width:] += go
            gb_ref[...] += gkv

    part = 2 * width // n
    cut = 2 * width // nx

    def copy_to(src, dst, where, sem):
        pltpu.make_async_remote_copy(
            src_ref=src,
            dst_ref=dst,
            send_sem=send_sem.at[sem],
            recv_sem=recv_sem.at[sem],
            device_id=where,
            device_id_type=MESH,
        ).start()

    def reduce_core():
        share = part // 2

        @pl.loop(0, n)
        def _(d):
            zz = d // PLANE
            yy = (d % PLANE) // 2
            cc = d % 2
            rows = pl.ds(pl.multiple_of(d * share, share), share)
            block = jnp.concatenate([ga_ref[rows, :], gb_ref[rows, :]], axis=0).astype(BF)
            at = pl.ds(pl.multiple_of((yy * nz + zz) * part, part), part)
            for k in range(nx):
                h1[cc, k, at, :] = block[:, k * cut : (k + 1) * cut]

        copy_to(h1.at[1 - c], r1, {"mem": me + 1 - 2 * c}, 5)

    def reduce_x():
        wait_got(r1, 5)
        for k in range(nx):
            h2[k] = (h1[c, k].astype(F32) + r1[k].astype(F32)).astype(BF)
        for k in range(1, nx):
            copy_to(h2.at[(x + k) % nx], r2.at[k - 1], {"rep": (x + k) % nx}, 6)

    def reduce_y():
        total = h2[x].astype(F32)
        if nx > 1:
            wait_got(r2, 6)
            for k in range(nx - 1):
                total = total + r2[k].astype(F32)
        h3[...] = total.astype(BF)
        length = nz * part
        for k in range(1, NY):
            yy = (y + k) % NY
            copy_to(
                h3.at[pl.ds(pl.multiple_of(yy * length, length), length)],
                r3.at[k - 1],
                {"mem": z * PLANE + yy * 2 + c},
                7,
            )

    def reduce_z():
        length = nz * part
        wait_got(r3, 7)
        total = h3[pl.ds(pl.multiple_of(y * length, length), length), :].astype(F32)
        for k in range(NY - 1):
            total = total + r3[k].astype(F32)
        h4[...] = total.astype(BF)
        for k in range(1, nz):
            zz = (z + k) % nz
            copy_to(
                h4.at[pl.ds(pl.multiple_of(zz * part, part), part)],
                r4.at[k - 1],
                {"mem": zz * PLANE + yc},
                8,
            )

    def share_x():
        total = h4[pl.ds(pl.multiple_of(z * part, part), part), :].astype(F32)
        if nz > 1:
            wait_got(r4, 8)
            for k in range(nz - 1):
                total = total + r4[k].astype(F32)
        fin[x] = total
        for k in range(1, nx):
            copy_to(fin.at[x], fin.at[x], {"rep": (x + k) % nx}, 9)

    def finish():
        if nx > 1:
            wait_got(fin.at[pl.ds(0, nx - 1)], 9)
        share = part // 2
        whole = jnp.concatenate([fin[k] for k in range(nx)], axis=1)
        gq_ref[...] = whole[:share, :width]
        go_ref[...] = whole[:share, width:]
        gkv_ref[...] = whole[share:, :]

    serve(0, mem_ref)
    prepare(0)
    prepare(1)
    fetch(0)
    update(0)
    attend(0)
    apply(0, mem_ref, mem1)
    serve(1, mem1)
    fetch(1)
    update(1)
    attend(1)
    reduce_core()
    reduce_x()
    apply(1, mem1, newmem_ref)
    reduce_y()
    reduce_z()
    share_x()
    finish()

    for b in range(2):
        wait_sent(served.at[b, pl.ds(0, slots - CAP)], 1 + b)
        wait_sent(outgoing.at[b, pl.ds(0, slots - CAP)], 3 + b)
    wait_sent(r1, 5)
    if nx > 1:
        wait_sent(r2, 6)
        wait_sent(fin.at[pl.ds(0, nx - 1)], 9)
    wait_sent(r3, 7)
    if nz > 1:
        wait_sent(r4, 8)


def on_device(
    memory,
    endpoint_owner,
    endpoint_row,
    event_time,
    neighbour_time,
    neighbour_feat,
    neighbour_index,
    valid_length,
    decay_rate,
    w_query,
    w_keyval,
    w_out,
    gru_input,
    gru_hidden,
    cotangent,
):
    n = lax.axis_size("mem")
    nx = lax.axis_size("rep")
    nz = n // PLANE
    _, nodes, width = memory.shape
    batches, events = event_time.shape[1:]
    nbrs = neighbour_time.shape[2]
    listed = neighbour_index.shape[3]
    ends = 2 * events
    slots = n * CAP
    part = 2 * width // n
    cut = 2 * width // nx
    owner = endpoint_owner[0].transpose(0, 2, 1).reshape(batches, ends)
    row = endpoint_row[0].transpose(0, 2, 1).reshape(batches, ends)
    vmem = pl.BlockSpec(memory_space=pltpu.VMEM)
    shape = jax.ShapeDtypeStruct
    share = width // n
    new_memory, embeddings, gq, gkv, go = pl.pallas_call(
        functools.partial(window, nx),
        out_shape=(
            shape((nodes, width), BF),
            shape((batches, events, width), BF),
            shape((share, width), F32),
            shape((share, 2 * width), F32),
            shape((share, width), F32),
        ),
        in_specs=[vmem] * 5 + [pl.BlockSpec(memory_space=pltpu.SMEM)] + [vmem] * 9,
        out_specs=(vmem,) * 5,
        scratch_shapes=[
            pltpu.VMEM((n, 1, 256), I32),
            pltpu.VMEM((n, 1, 256), I32),
            pltpu.VMEM((batches, slots, width), BF),
            pltpu.VMEM((batches, slots, width), BF),
            pltpu.VMEM((batches, slots, width), BF),
            pltpu.VMEM((batches, slots, width), BF),
            pltpu.VMEM((nodes, width), BF),
            pltpu.VMEM((8, ends), I32),
            pltpu.VMEM((8, slots), I32),
            pltpu.VMEM((batches, slots, 128), I32),
            pltpu.VMEM((batches, ends, slots), BF),
            pltpu.VMEM((batches, 2, events, width), BF),
            pltpu.VMEM((ends, width), BF),
            pltpu.VMEM((listed, events), I32),
            pltpu.VMEM((batches, nbrs, events), F32),
            pltpu.VMEM((batches, nbrs, events), F32),
            pltpu.VMEM((batches, nbrs, 2 * width), BF),
            pltpu.VMEM((batches, 2 * width, nbrs), BF),
            pltpu.VMEM((events, width), BF),
            pltpu.VMEM((events, width), BF),
            pltpu.VMEM((width, events), BF),
            pltpu.VMEM((width, events), BF),
            pltpu.VMEM((nbrs, 2 * width), BF),
            pltpu.VMEM((width, 2 * width), F32),
            pltpu.VMEM((width, 2 * width), F32),
            pltpu.VMEM((2, nx, n // 2 * part, cut), BF),
            pltpu.VMEM((nx, n // 2 * part, cut), BF),
            pltpu.VMEM((nx, n // 2 * part, cut), BF),
            pltpu.VMEM((max(nx - 1, 1), n // 2 * part, cut), BF),
            pltpu.VMEM((n // 2 * part, cut), BF),
            pltpu.VMEM((NY - 1, nz * part, cut), BF),
            pltpu.VMEM((nz * part, cut), BF),
            pltpu.VMEM((max(nz - 1, 1), part, cut), BF),
            pltpu.VMEM((nx, part, cut), F32),
            pltpu.SemaphoreType.DMA((10,)),
            pltpu.SemaphoreType.DMA((10,)),
        ],
        compiler_params=pltpu.CompilerParams(
            collective_id=0, has_side_effects=True, vmem_limit_bytes=60 * 1024 * 1024
        ),
        name="window",
    )(
        owner,
        row,
        event_time[0],
        neighbour_time[0],
        valid_length[0],
        decay_rate,
        neighbour_index[0],
        memory[0],
        neighbour_feat[0],
        cotangent[0],
        w_query,
        w_keyval,
        w_out,
        gru_input,
        gru_hidden,
    )
    return (new_memory[None], embeddings[None], gq, gkv, go)


def solution(mesh):
    return jax.shard_map(
        on_device,
        mesh=mesh,
        in_specs=(
            P("rep", "mem", None),
            P("rep", None, "mem", None),
            P("rep", None, "mem", None),
            P("rep", None, "mem"),
            P("rep", None, "mem"),
            P("rep", None, "mem", None),
            P("rep", None, "mem", None),
            P("rep", None, "mem"),
            P(),
            P(),
            P(),
            P(),
            P(),
            P(),
            P("rep", None, "mem", None),
        ),
        out_specs=(
            P("rep", "mem", None),
            P("rep", None, "mem", None),
            P("mem", None),
            P("mem", None),
            P("mem", None),
        ),
        check_vma=False,
    )
```

```python
import functools
import math

import jax
import jax.numpy as jnp
from jax import lax
from jax.experimental import pallas as pl
from jax.experimental.pallas import tpu as pltpu
from jax.sharding import PartitionSpec as P

MESH = pl.DeviceIdType.MESH
BF = jnp.bfloat16
F32 = jnp.float32
I32 = jnp.int32
CAP = 16
PLANE = 8
GROUP = CAP * PLANE
HEADS = 8
NY = 4


def nn(a, b):
    return lax.dot_general(a, b, (((1,), (0,)), ((), ())), preferred_element_type=F32)


def nt(a, b):
    return lax.dot_general(a, b, (((1,), (1,)), ((), ())), preferred_element_type=F32)


def sigmoid(a):
    return 0.5 * jnp.tanh(0.5 * a) + 0.5


def iota(shape, axis):
    return lax.broadcasted_iota(I32, shape, axis)


def one_hot(mask):
    return jnp.where(mask, 1.0, 0.0).astype(BF)


def window(
    nx,
    owner_ref,
    row_ref,
    et_ref,
    nt_ref,
    vl_ref,
    decay_ref,
    nidx_hbm,
    mem_hbm,
    feat_hbm,
    cot_hbm,
    wq_hbm,
    wkv_hbm,
    wo_hbm,
    gi_hbm,
    gh_hbm,
    newmem_hbm,
    emb_hbm,
    gq_ref,
    gkv_ref,
    go_ref,
    nidx_ref,
    mem_ref,
    feat_ref,
    cot_ref,
    wq_ref,
    wkv_ref,
    wo_ref,
    gi_ref,
    gh_ref,
    newmem_ref,
    emb_ref,
    in_sem,
    out_sem,
    ids_out,
    ids_in,
    served,
    answered,
    outgoing,
    arrived,
    mem1,
    slot_ref,
    lane_ref,
    col_ref,
    pick_ref,
    pickt_ref,
    asked_ref,
    named_ref,
    inverse_ref,
    rows_ref,
    upd_ref,
    idx_ref,
    mult_ref,
    bias_ref,
    dw_ref,
    kv_ref,
    kvt_ref,
    q_ref,
    datt_ref,
    att_ref,
    dq_ref,
    dkv_ref,
    ga_ref,
    gb_ref,
    h1,
    r1,
    h2,
    r2,
    h3,
    r3,
    h4,
    r4,
    send_sem,
    recv_sem,
):
    n = ids_in.shape[0]
    nz = n // PLANE
    nodes, width = mem_ref.shape
    events = et_ref.shape[1]
    nbrs = nt_ref.shape[1]
    ends = 2 * events
    slots = n * CAP
    wide = width // 2
    me = lax.axis_index("mem")
    x = lax.axis_index("rep")
    z = me // PLANE
    yc = me % PLANE
    y = yc // 2
    c = yc % 2

    loads = {}
    for at, (name, src, dst) in enumerate(
        (
            ("mem", mem_hbm, mem_ref),
            ("nidx", nidx_hbm, nidx_ref),
            ("feat", feat_hbm, feat_ref),
            ("wkv", wkv_hbm, wkv_ref),
            ("gi", gi_hbm, gi_ref),
            ("gh", gh_hbm, gh_ref),
            ("wq", wq_hbm, wq_ref),
            ("wo", wo_hbm, wo_ref),
            ("cot", cot_hbm, cot_ref),
        )
    ):
        loads[name] = pltpu.make_async_copy(src, dst, in_sem.at[at])
        loads[name].start()

    def loaded(*names):
        for name in names:
            loads[name].wait()

    barrier = pltpu.get_barrier_semaphore()

    @pl.loop(1, n)
    def _(k):
        pl.semaphore_signal(barrier, inc=1, device_id={"mem": (me + k) % n}, device_id_type=MESH)

    for k in range(1, nx):
        pl.semaphore_signal(barrier, inc=1, device_id={"rep": (x + k) % nx}, device_id_type=MESH)

    @pl.loop(1, nz)
    def _(k):
        for j in range(1, nx):
            pl.semaphore_signal(
                barrier,
                inc=1,
                device_id={"mem": (z + k) % nz * PLANE + yc, "rep": (x + j) % nx},
                device_id_type=MESH,
            )

    def group_at(i):
        h = (i + 1) // 2
        return nz // 2 + h * (1 - 2 * (i % 2))

    def start_group(src, dst, g, sem):
        @pl.loop(0, PLANE)
        def _(j):
            @pl.when(g * PLANE + j > 0)
            def _():
                q = g * PLANE + (j + yc) % PLANE
                other = (q + z * PLANE) % n
                mine = (me + n - (other // PLANE) * PLANE) % n
                pltpu.make_async_remote_copy(
                    src_ref=src(q),
                    dst_ref=dst(mine),
                    send_sem=send_sem.at[sem],
                    recv_sem=recv_sem.at[sem],
                    device_id={"mem": other},
                    device_id_type=MESH,
                ).start()

    def columns(t):
        return pl.ds(t * wide, wide)

    def block(ref, b, t):
        return lambda q: ref.at[b, pl.ds(pl.multiple_of(q * CAP, CAP), CAP), columns(t)]

    def own_block(src, dst, b, t):
        here = pl.ds(pl.multiple_of(yc * CAP, CAP), CAP)
        dst[b, here, columns(t)] = src[b, here, columns(t)]

    def others(ref, b, t):
        return ref.at[b, pl.ds(0, slots - CAP), columns(t)]

    def wait_sent(view, sem):
        pltpu.make_async_copy(view, view, send_sem.at[sem]).wait()

    def wait_got(view, sem):
        pltpu.make_async_copy(view, view, recv_sem.at[sem]).wait()

    before = one_hot(iota((ends, ends), 0) < iota((ends, ends), 1))
    for b in range(2):
        own = jnp.concatenate([owner_ref[b, 0:1, :], owner_ref[b, 1:2, :]], axis=1) - z * PLANE
        own = jnp.where(own < 0, own + n, own)
        marks = jnp.where(iota((n, ends), 0) == own, 1.0, 0.0)
        marks_bf = marks.astype(BF)
        rank = jnp.sum(nn(marks_bf, before) * marks, axis=0, keepdims=True).astype(I32)
        slot_ref[b : b + 1, :] = own * CAP + rank
        wanted = jnp.concatenate([row_ref[b, 0:1, :], row_ref[b, 1:2, :]], axis=1) + 1
        here = (iota((128, ends), 0) % CAP) == rank
        high = jnp.where(here, (wanted // 64).astype(F32), 0.0).astype(BF)
        low = jnp.where(here, (wanted % 64).astype(F32), 0.0).astype(BF)
        found = nt(marks_bf, high) * 64.0 + nt(marks_bf, low)
        ids_out[:, :, b * 128 : (b + 1) * 128] = (found.astype(I32) - 1).reshape(n, 1, 128)

    pl.semaphore_wait(barrier, n - 1 + (nx - 1) * nz)

    @pl.loop(0, nz)
    def _(i):
        start_group(lambda q: ids_out.at[pl.ds(q, 1)], lambda q: ids_in.at[pl.ds(q, 1)], group_at(i), 0)

    ids_in[pl.ds(yc, 1)] = ids_out[pl.ds(yc, 1)]
    wait_got(ids_in.at[pl.ds(0, n - 1)], 0)
    wait_sent(ids_out.at[pl.ds(0, n - 1)], 0)

    for b in range(2):
        seen = ids_in[:, :, b * 128 : (b + 1) * 128].reshape(n, 128).astype(F32)
        mine = (iota((n, 128), 0) % PLANE) == (iota((n, 128), 1) // CAP)
        packed = jnp.sum(jnp.where(mine, seen, 0.0).reshape(nz, PLANE, 128), axis=1)
        for g in range(nz):
            row = packed[g : g + 1, :]
            lane_ref[b : b + 1, g * GROUP : (g + 1) * GROUP] = row.astype(I32)
            col_ref[b, g * GROUP : (g + 1) * GROUP, :] = jnp.broadcast_to(row, (128, 128)).T.astype(I32)

    per = 2 if nz % 2 == 0 else 1

    def places(i):
        groups = [group_at(per * i + t) for t in range(per)]
        return groups, [pl.ds(pl.multiple_of(g * GROUP, GROUP), GROUP) for g in groups]

    def ask(b, where):
        wanted = jnp.concatenate([col_ref[b, at, 0:1] for at in where], axis=0)
        pick = one_hot(wanted == iota((per * GROUP, nodes), 1))
        for t in range(per):
            asked_ref[where[t], :] = pick[t * GROUP : (t + 1) * GROUP]
        return pick

    def ask_all(b):
        @pl.loop(0, nz // per)
        def _(i):
            ask(b, places(i)[1])

    def serve(b, t, source):
        @pl.loop(0, nz // per)
        def _(i):
            groups, where = places(i)
            if b == 0 and t == 0:
                pick = ask(b, where)
            else:
                pick = jnp.concatenate([asked_ref[at, :] for at in where], axis=0)
            got = nn(pick, source[:, columns(t)]).astype(BF)
            for k in range(per):
                served[b, where[k], columns(t)] = got[k * GROUP : (k + 1) * GROUP]
            for k in range(per):
                start_group(block(served, b, t), block(answered, b, t), groups[k], 1 + 2 * b + t)

        own_block(served, answered, b, t)

    def prepare(b):
        kv = nn(feat_ref[b], wkv_ref[...]).astype(BF)
        kv_ref[...] = kv
        kvt_ref[...] = kv.T
        datt_ref[...] = nt(cot_ref[b], wo_ref[...]).astype(BF)
        slot_row = slot_ref[b : b + 1, :]
        slot_col = jnp.broadcast_to(slot_row.astype(F32), (128, ends)).T.astype(I32)
        pick_ref[...] = one_hot(slot_col[:, 0:1] == iota((ends, slots), 1))
        pickt_ref[...] = one_hot(iota((slots, ends), 0) == slot_row)
        listed = nidx_ref[b].astype(F32).T
        count = listed.shape[0]
        idx_ref[...] = jnp.where(iota((count, events), 0) < vl_ref[b : b + 1, :], listed, -1.0).astype(I32)
        step = min(64, nbrs)

        @pl.loop(0, nbrs // step)
        def _(k):
            place = iota((step, events), 0) + k * step

            def add(j, total):
                rows = idx_ref[pl.ds(pl.multiple_of(j * 8, 8), 8), :]
                for t in range(8):
                    total = total + jnp.where(place == rows[t : t + 1, :], 1.0, 0.0)
                return total

            mult_ref[pl.ds(pl.multiple_of(k * step, step), step), :] = lax.fori_loop(
                0, count // 8, add, jnp.zeros((step, events), F32)
            )

        since = jnp.broadcast_to(nt_ref[b : b + 1, :].astype(F32), (128, nbrs)).T
        elapsed = jnp.log(1.0 + (et_ref[b : b + 1, :].astype(F32) - since[:, 0:1]))
        mult = mult_ref[...]
        level = jnp.where(mult > 0, jnp.log(jnp.maximum(mult, 1.0)), -1e30)
        for head in range(HEADS):
            bias_ref[head] = level - decay_ref[head] * elapsed
            d = datt_ref[:, pair_columns(head // 2)] * half_lanes(head % 2, 1.0)
            dw_ref[head] = nt(kv_ref[:, pair_columns(head // 2, width)], d)

    half_width = width // HEADS

    def pair_columns(pair, base=0):
        return pl.ds(base + pair * 2 * half_width, 2 * half_width)

    def half_lanes(half, value):
        return jnp.where(iota((1, 2 * half_width), 1) // half_width == half, value, 0.0).astype(BF)

    step = min(512, nodes)

    def name_rows(b):
        @pl.loop(0, nodes // step)
        def _(k):
            at = pl.ds(pl.multiple_of(k * step, step), step)
            marks = jnp.where(iota((step, slots), 0) + k * step == lane_ref[b : b + 1, :], 1.0, 0.0)
            counts = jnp.sum(marks, axis=1, keepdims=True)
            named_ref[at, :] = marks.astype(BF)
            inverse = jnp.where(counts > 0, 1.0 / jnp.maximum(counts, 1.0), 0.0)
            inverse_ref[at, :] = jnp.broadcast_to(inverse, (step, 128))

    def fetch(b):
        for t in range(2):
            wait_got(others(answered, b, t), 1 + 2 * b + t)
            got = nn(pick_ref[...], answered[b, :, columns(t)]).astype(BF)
            rows_ref[b, 0, :, columns(t)] = got[:events]
            rows_ref[b, 1, :, columns(t)] = got[events:]

    def update(b):
        for t in range(2):

            @pl.loop(0, 2)
            def _(k):
                state = rows_ref[b, k]
                partner = rows_ref[b, 1 - k]
                part = [slice(i * width + t * wide, i * width + (t + 1) * wide) for i in range(3)]
                reset = sigmoid(nn(partner, gi_ref[:, part[0]]) + nn(state, gh_ref[:, part[0]]))
                keep = sigmoid(nn(partner, gi_ref[:, part[1]]) + nn(state, gh_ref[:, part[1]]))
                candidate = jnp.tanh(nn(partner, gi_ref[:, part[2]]) + reset * nn(state, gh_ref[:, part[2]]))
                old = rows_ref[b, k, :, columns(t)].astype(F32)
                upd_ref[pl.ds(pl.multiple_of(k * events, events), events), columns(t)] = (
                    candidate + keep * (old - candidate)
                ).astype(BF)

            @pl.loop(0, nz // per)
            def _(i):
                groups, where = places(i)
                pick = jnp.concatenate([pickt_ref[at, :] for at in where], axis=0)
                got = nn(pick, upd_ref[:, columns(t)]).astype(BF)
                for k in range(per):
                    outgoing[b, where[k], columns(t)] = got[k * GROUP : (k + 1) * GROUP]
                for k in range(per):
                    start_group(block(outgoing, b, t), block(arrived, b, t), groups[k], 5 + 2 * b + t)

            own_block(outgoing, arrived, b, t)

    def apply(b, t, source, target):
        wait_got(others(arrived, b, t), 5 + 2 * b + t)

        @pl.loop(0, nodes // step)
        def _(k):
            at = pl.ds(pl.multiple_of(k * step, step), step)
            sums = nn(named_ref[at, :], arrived[b, :, columns(t)])
            inverse = inverse_ref[at, 0:1]
            old = source[at, columns(t)].astype(F32)
            target[at, columns(t)] = jnp.where(inverse > 0, sums * inverse, old).astype(BF)

    def store_memory(k):
        at = pl.ds(k * step, step)
        return pltpu.make_async_copy(newmem_ref.at[at], newmem_hbm.at[at], out_sem.at[2 + k])

    def store_embeddings(b):
        return pltpu.make_async_copy(emb_ref.at[b], emb_hbm.at[b], out_sem.at[b])

    def attend(b):
        source = rows_ref[b, 0]
        cot = cot_ref[b]
        q_ref[...] = nn(source, wq_ref[...]).astype(BF)
        scale = 1.0 / math.sqrt(half_width)

        for pair in range(HEADS // 2):
            cols = pair_columns(pair)
            vcols = pair_columns(pair, width)
            dk = jnp.zeros((nbrs, 2 * half_width), F32)
            dv = jnp.zeros((nbrs, 2 * half_width), F32)
            for half in range(2):
                head = 2 * pair + half
                q = q_ref[:, cols] * half_lanes(half, scale)
                d = datt_ref[:, cols] * half_lanes(half, 1.0)
                logits = nt(kv_ref[:, cols], q) + bias_ref[head]
                weighted = jnp.exp(logits - jnp.max(logits, axis=0, keepdims=True))
                weights = weighted * (1.0 / jnp.sum(weighted, axis=0, keepdims=True))
                w = weights.astype(BF)
                at = pl.ds(head * half_width, half_width)
                vat = pl.ds(width + head * half_width, half_width)
                att_ref[at, :] = nn(kvt_ref[vat, :], w).astype(BF)
                dw = dw_ref[head]
                inner = jnp.sum(dw * weights, axis=0, keepdims=True)
                dl = (weights * (dw - inner)).astype(BF)
                dq_ref[at, :] = (nn(kvt_ref[at, :], dl) * scale).astype(BF)
                dv = dv + nn(w, d)
                dk = dk + nn(dl, q)
            dkv_ref[:, cols] = dk.astype(BF)
            dkv_ref[:, vcols] = dv.astype(BF)

        emb_ref[b] = (source.astype(F32) + nn(att_ref[...].T, wo_ref[...])).astype(BF)
        go = nn(att_ref[...], cot)
        gq = nn(source.T, dq_ref[...].T)
        gkv = nn(feat_ref[b].T, dkv_ref[...])
        if b == 0:
            ga_ref[:, :width] = gq
            ga_ref[:, width:] = go
            gb_ref[...] = gkv
        else:
            ga_ref[:, :width] += gq
            ga_ref[:, width:] += go
            gb_ref[...] += gkv

    part = 2 * width // n
    plane = nz * part
    cut = width // nx

    def copy_to(src, dst, where, sem):
        pltpu.make_async_remote_copy(
            src_ref=src,
            dst_ref=dst,
            send_sem=send_sem.at[sem],
            recv_sem=recv_sem.at[sem],
            device_id=where,
            device_id_type=MESH,
        ).start()

    def rows_of_y(k):
        return pl.ds(pl.multiple_of(k * plane, plane), plane)

    def rows_of_z(k):
        return pl.ds(pl.multiple_of(k * part, part), part)

    def reduce_core(t):
        share = part // 2

        @pl.loop(0, n)
        def _(d):
            zz = d // PLANE
            yy = (d % PLANE) // 2
            cc = d % 2
            rows = pl.ds(pl.multiple_of(d * share, share), share)
            cols = pl.ds(t * width, width)
            both = jnp.concatenate([ga_ref[rows, cols], gb_ref[rows, cols]], axis=0).astype(BF)
            at = pl.ds(pl.multiple_of((yy * nz + zz) * part, part), part)
            for k in range(nx):
                h1[t, cc, k, at, :] = both[:, k * cut : (k + 1) * cut]

        copy_to(h1.at[t, 1 - c], r1.at[t], {"mem": me + 1 - 2 * c}, 9 + t)

    def reduce_x(t):
        wait_got(r1.at[t], 9 + t)
        for k in range(nx):
            h2[t, k] = (h1[t, c, k].astype(F32) + r1[t, k].astype(F32)).astype(BF)
        for k in range(1, nx):
            xx = (x + k) % nx
            copy_to(h2.at[t, xx], r2.at[t, k - 1], {"rep": xx}, 11 + t)

    def reduce_y(t):
        total = h2[t, x].astype(F32)
        if nx > 1:
            wait_got(r2.at[t], 11 + t)
            for k in range(nx - 1):
                total = total + r2[t, k].astype(F32)
        h3[t] = total.astype(BF)
        for k in range(1, NY):
            yy = (y + k) % NY
            copy_to(h3.at[t, rows_of_y(yy)], r3.at[t, k - 1], {"mem": z * PLANE + yy * 2 + c}, 13 + t)

    def reduce_z():
        for t in range(2):
            wait_got(r3.at[t], 13 + t)
            total = h3[t, rows_of_y(y), :].astype(F32)
            for k in range(NY - 1):
                total = total + r3[t, k].astype(F32)
            h4[:, t * cut : (t + 1) * cut] = total.astype(BF)
        here = r4.at[z * nx + x]
        here[...] = h4[rows_of_z(z), :]
        for k in range(1, nx):
            copy_to(h4.at[rows_of_z(z)], here, {"rep": (x + k) % nx}, 15)

        @pl.loop(1, nz)
        def _(k):
            zz = (z + k) % nz
            for j in range(nx):
                there = {"mem": zz * PLANE + yc, "rep": (x + j) % nx} if j else {"mem": zz * PLANE + yc}
                copy_to(h4.at[rows_of_z(zz)], here, there, 15)

    def all_but_one():
        return r4.at[pl.ds(0, nz * nx - 1)]

    def finish():
        wait_got(all_but_one(), 15)
        share = part // 2
        for k in range(nx):
            total = r4[k].astype(F32)
            for j in range(1, nz):
                total = total + r4[j * nx + k].astype(F32)
            at = slice(k * cut, (k + 1) * cut)
            gq_ref[:, at] = total[:share, :cut]
            go_ref[:, at] = total[:share, cut:]
            gkv_ref[:, at] = total[share:, :cut]
            gkv_ref[:, width + k * cut : width + (k + 1) * cut] = total[share:, cut:]

    loaded("mem")
    serve(0, 0, mem_ref)
    serve(0, 1, mem_ref)
    loaded("nidx", "feat", "wkv", "wo", "cot")
    prepare(0)
    name_rows(0)
    ask_all(1)
    loaded("gi", "gh", "wq")
    fetch(0)
    update(0)
    attend(0)
    store_embeddings(0).start()
    for t in range(2):
        apply(0, t, mem_ref, mem1)
        serve(1, t, mem1)
    prepare(1)
    name_rows(1)
    fetch(1)
    update(1)
    attend(1)
    store_embeddings(1).start()
    reduce_core(0)
    reduce_core(1)
    reduce_x(0)
    reduce_x(1)
    apply(1, 0, mem1, newmem_ref)
    reduce_y(0)
    reduce_y(1)
    reduce_z()
    apply(1, 1, mem1, newmem_ref)
    for k in range(nodes // step):
        store_memory(k).start()
    finish()

    for b in range(2):
        for t in range(2):
            wait_sent(others(served, b, t), 1 + 2 * b + t)
            wait_sent(others(outgoing, b, t), 5 + 2 * b + t)
        store_embeddings(b).wait()
    for t in range(2):
        wait_sent(r1.at[t], 9 + t)
        if nx > 1:
            wait_sent(r2.at[t], 11 + t)
        wait_sent(r3.at[t], 13 + t)
    wait_sent(all_but_one(), 15)
    for k in range(nodes // step):
        store_memory(k).wait()


def hand_on(*refs):
    count = (len(refs) - 1) // 3
    sem = refs[-1]
    steps = []
    for src, dst, held in zip(refs[:count], refs[count : 2 * count], refs[2 * count : 3 * count]):
        rows = src.shape[0]
        pieces = 4 if rows % 128 == 0 else 1
        for k in range(pieces):
            at = pl.ds(k * (rows // pieces), rows // pieces)
            get = pltpu.make_async_copy(src.at[at], held.at[at], sem.at[0, len(steps)])
            put = pltpu.make_async_copy(held.at[at], dst.at[at], sem.at[1, len(steps)])
            get.start()
            steps.append((get, put))
    for get, put in steps:
        get.wait()
        put.start()
    for _, put in steps:
        put.wait()


def on_device(
    memory,
    endpoint_owner,
    endpoint_row,
    event_time,
    neighbour_time,
    neighbour_feat,
    neighbour_index,
    valid_length,
    decay_rate,
    w_query,
    w_keyval,
    w_out,
    gru_input,
    gru_hidden,
    cotangent,
):
    n = lax.axis_size("mem")
    nx = lax.axis_size("rep")
    nz = n // PLANE
    _, nodes, width = memory.shape
    batches, events = event_time.shape[1:]
    nbrs = neighbour_time.shape[2]
    listed = neighbour_index.shape[3]
    ends = 2 * events
    slots = n * CAP
    part = 2 * width // n
    plane = nz * part
    half = n // 2 * part
    cut = width // nx
    owner = endpoint_owner[0].transpose(0, 2, 1)
    row = endpoint_row[0].transpose(0, 2, 1)
    vmem = pl.BlockSpec(memory_space=pltpu.VMEM)
    shape = jax.ShapeDtypeStruct
    share = width // n
    hbm = pl.BlockSpec(memory_space=pl.ANY)
    outputs = (
        shape((nodes, width), BF),
        shape((batches, events, width), BF),
        shape((share, width), F32),
        shape((share, 2 * width), F32),
        shape((share, width), F32),
    )
    results = pl.pallas_call(
        functools.partial(window, nx),
        out_shape=outputs,
        in_specs=[vmem] * 5 + [pl.BlockSpec(memory_space=pltpu.SMEM)] + [hbm] * 9,
        out_specs=(hbm,) * 2 + (vmem,) * 3,
        scratch_shapes=[
            pltpu.VMEM((batches, events, listed), I32),
            pltpu.VMEM((nodes, width), BF),
            pltpu.VMEM((batches, nbrs, width), BF),
            pltpu.VMEM((batches, events, width), BF),
            pltpu.VMEM((width, width), BF),
            pltpu.VMEM((width, 2 * width), BF),
            pltpu.VMEM((width, width), BF),
            pltpu.VMEM((width, 3 * width), BF),
            pltpu.VMEM((width, 3 * width), BF),
            pltpu.VMEM((nodes, width), BF),
            pltpu.VMEM((batches, events, width), BF),
            pltpu.SemaphoreType.DMA((9,)),
            pltpu.SemaphoreType.DMA((2 + nodes // min(512, nodes),)),
            pltpu.VMEM((n, 1, 256), I32),
            pltpu.VMEM((n, 1, 256), I32),
            pltpu.VMEM((batches, slots, width), BF),
            pltpu.VMEM((batches, slots, width), BF),
            pltpu.VMEM((batches, slots, width), BF),
            pltpu.VMEM((batches, slots, width), BF),
            pltpu.VMEM((nodes, width), BF),
            pltpu.VMEM((8, ends), I32),
            pltpu.VMEM((8, slots), I32),
            pltpu.VMEM((batches, slots, 128), I32),
            pltpu.VMEM((ends, slots), BF),
            pltpu.VMEM((slots, ends), BF),
            pltpu.VMEM((slots, nodes), BF),
            pltpu.VMEM((nodes, slots), BF),
            pltpu.VMEM((nodes, 128), F32),
            pltpu.VMEM((batches, 2, events, width), BF),
            pltpu.VMEM((ends, width), BF),
            pltpu.VMEM((listed, events), I32),
            pltpu.VMEM((nbrs, events), F32),
            pltpu.VMEM((HEADS, nbrs, events), F32),
            pltpu.VMEM((HEADS, nbrs, events), F32),
            pltpu.VMEM((nbrs, 2 * width), BF),
            pltpu.VMEM((2 * width, nbrs), BF),
            pltpu.VMEM((events, width), BF),
            pltpu.VMEM((events, width), BF),
            pltpu.VMEM((width, events), BF),
            pltpu.VMEM((width, events), BF),
            pltpu.VMEM((nbrs, 2 * width), BF),
            pltpu.VMEM((width, 2 * width), F32),
            pltpu.VMEM((width, 2 * width), F32),
            pltpu.VMEM((2, 2, nx, half, cut), BF),
            pltpu.VMEM((2, nx, half, cut), BF),
            pltpu.VMEM((2, nx, half, cut), BF),
            pltpu.VMEM((2, max(nx - 1, 1), half, cut), BF),
            pltpu.VMEM((2, half, cut), BF),
            pltpu.VMEM((2, NY - 1, plane, cut), BF),
            pltpu.VMEM((plane, 2 * cut), BF),
            pltpu.VMEM((nz * nx, part, 2 * cut), BF),
            pltpu.SemaphoreType.DMA((16,)),
            pltpu.SemaphoreType.DMA((16,)),
        ],
        compiler_params=pltpu.CompilerParams(
            collective_id=0, has_side_effects=True, vmem_limit_bytes=60 * 1024 * 1024
        ),
        name="window",
    )(
        owner,
        row,
        event_time[0],
        neighbour_time[0],
        valid_length[0],
        decay_rate,
        neighbour_index[0],
        memory[0],
        neighbour_feat[0],
        cotangent[0],
        w_query,
        w_keyval,
        w_out,
        gru_input,
        gru_hidden,
    )
    new_memory, embeddings, gq, gkv, go = pl.pallas_call(
        hand_on,
        out_shape=outputs,
        in_specs=[hbm] * 5,
        out_specs=(hbm,) * 5,
        scratch_shapes=[pltpu.VMEM(out.shape, out.dtype) for out in outputs] + [pltpu.SemaphoreType.DMA((2, 8))],
        compiler_params=pltpu.CompilerParams(vmem_limit_bytes=60 * 1024 * 1024),
        name="hand_on",
    )(*results)
    return (new_memory[None], embeddings[None], gq, gkv, go)


def solution(mesh):
    return jax.shard_map(
        on_device,
        mesh=mesh,
        in_specs=(
            P("rep", "mem", None),
            P("rep", None, "mem", None),
            P("rep", None, "mem", None),
            P("rep", None, "mem"),
            P("rep", None, "mem"),
            P("rep", None, "mem", None),
            P("rep", None, "mem", None),
            P("rep", None, "mem"),
            P(),
            P(),
            P(),
            P(),
            P(),
            P(),
            P("rep", None, "mem", None),
        ),
        out_specs=(
            P("rep", "mem", None),
            P("rep", None, "mem", None),
            P("mem", None),
            P("mem", None),
            P("mem", None),
        ),
        check_vma=False,
    )
```

```python
import functools
import math

import jax
import jax.numpy as jnp
from jax import lax
from jax.experimental import pallas as pl
from jax.experimental.pallas import tpu as pltpu
from jax.sharding import PartitionSpec as P

MESH = pl.DeviceIdType.MESH
BF = jnp.bfloat16
F32 = jnp.float32
I32 = jnp.int32
CAP = 16
PLANE = 8
GROUP = CAP * PLANE
HEADS = 8
NY = 4


def nn(a, b):
    return lax.dot_general(a, b, (((1,), (0,)), ((), ())), preferred_element_type=F32)


def nt(a, b):
    return lax.dot_general(a, b, (((1,), (1,)), ((), ())), preferred_element_type=F32)


def sigmoid(a):
    return 0.5 * jnp.tanh(0.5 * a) + 0.5


def iota(shape, axis):
    return lax.broadcasted_iota(I32, shape, axis)


def one_hot(mask):
    return jnp.where(mask, 1.0, 0.0).astype(BF)


def window(
    nx,
    owner_ref,
    row_ref,
    et_ref,
    nt_ref,
    vl_ref,
    decay_ref,
    nidx_hbm,
    mem_hbm,
    feat_hbm,
    cot_hbm,
    wq_hbm,
    wkv_hbm,
    wo_hbm,
    gi_hbm,
    gh_hbm,
    newmem_hbm,
    emb_hbm,
    gq_ref,
    gkv_ref,
    go_ref,
    nidx_ref,
    mem_ref,
    feat_ref,
    cot_ref,
    wq_ref,
    wkv_ref,
    wo_ref,
    gi_ref,
    gh_ref,
    newmem_ref,
    emb_ref,
    in_sem,
    out_sem,
    ids_out,
    ids_in,
    served,
    answered,
    outgoing,
    arrived,
    mem1,
    slot_ref,
    lane_ref,
    col_ref,
    pick_ref,
    pickt_ref,
    asked_ref,
    named_ref,
    inverse_ref,
    rows_ref,
    upd_ref,
    idx_ref,
    mult_ref,
    bias_ref,
    dw_ref,
    kv_ref,
    kvt_ref,
    q_ref,
    datt_ref,
    att_ref,
    dq_ref,
    dkv_ref,
    ga_ref,
    gb_ref,
    h1,
    r1,
    h2,
    r2,
    h3,
    r3,
    h4,
    r4,
    fin,
    send_sem,
    recv_sem,
):
    n = ids_in.shape[0]
    nz = n // PLANE
    nodes, width = mem_ref.shape
    events = et_ref.shape[1]
    nbrs = nt_ref.shape[1]
    ends = 2 * events
    slots = n * CAP
    wide = width // 2
    me = lax.axis_index("mem")
    x = lax.axis_index("rep")
    z = lax.div(me, PLANE)
    yc = lax.rem(me, PLANE)
    y = lax.div(yc, 2)
    c = lax.rem(yc, 2)

    loads = {}
    for at, (name, src, dst) in enumerate(
        (
            ("mem", mem_hbm, mem_ref),
            ("nidx", nidx_hbm, nidx_ref),
            ("feat", feat_hbm, feat_ref),
            ("wkv", wkv_hbm, wkv_ref),
            ("gi", gi_hbm, gi_ref),
            ("gh", gh_hbm, gh_ref),
            ("wq", wq_hbm, wq_ref),
            ("wo", wo_hbm, wo_ref),
            ("cot", cot_hbm, cot_ref),
        )
    ):
        loads[name] = pltpu.make_async_copy(src, dst, in_sem.at[at])
        loads[name].start()

    def loaded(*names):
        for name in names:
            loads[name].wait()

    barrier = pltpu.get_barrier_semaphore()

    @pl.loop(1, n)
    def _(k):
        pl.semaphore_signal(barrier, inc=1, device_id={"mem": lax.rem(me + k, n)}, device_id_type=MESH)

    for k in range(1, nx):
        pl.semaphore_signal(barrier, inc=1, device_id={"rep": (x + k) % nx}, device_id_type=MESH)

    def group_at(i):
        h = lax.div(i + 1, 2)
        return nz // 2 + h * (1 - 2 * lax.rem(i, 2))

    def start_group(src, dst, g, sem):
        there = lax.rem(g + z, nz) * PLANE
        mine = lax.rem(nz - g, nz) * PLANE + yc
        for j in range(PLANE):
            turned = lax.rem(yc + j, PLANE)

            def send(turned=turned):
                pltpu.make_async_remote_copy(
                    src_ref=src(g * PLANE + turned),
                    dst_ref=dst(mine),
                    send_sem=send_sem.at[sem],
                    recv_sem=recv_sem.at[sem],
                    device_id={"mem": there + turned},
                    device_id_type=MESH,
                ).start()

            if j:
                send()
            else:
                pl.when(g > 0)(send)

    def columns(t):
        return pl.ds(t * wide, wide)

    def block(ref, b, t):
        return lambda q: ref.at[b, pl.ds(pl.multiple_of(q * CAP, CAP), CAP), columns(t)]

    def own_block(src, dst, b, t):
        here = pl.ds(pl.multiple_of(yc * CAP, CAP), CAP)
        dst[b, here, columns(t)] = src[b, here, columns(t)]

    def others(ref, b, t):
        return ref.at[b, pl.ds(0, slots - CAP), columns(t)]

    def wait_sent(view, sem):
        pltpu.make_async_copy(view, view, send_sem.at[sem]).wait()

    def wait_got(view, sem):
        pltpu.make_async_copy(view, view, recv_sem.at[sem]).wait()

    before = one_hot(iota((ends, ends), 0) < iota((ends, ends), 1))
    for b in range(2):
        own = jnp.concatenate([owner_ref[b, 0:1, :], owner_ref[b, 1:2, :]], axis=1) - z * PLANE
        own = jnp.where(own < 0, own + n, own)
        marks = jnp.where(iota((n, ends), 0) == own, 1.0, 0.0)
        marks_bf = marks.astype(BF)
        rank = jnp.sum(nn(marks_bf, before) * marks, axis=0, keepdims=True).astype(I32)
        slot_ref[b : b + 1, :] = own * CAP + rank
        wanted = jnp.concatenate([row_ref[b, 0:1, :], row_ref[b, 1:2, :]], axis=1) + 1
        here = (iota((128, ends), 0) % CAP) == rank
        high = jnp.where(here, (wanted // 64).astype(F32), 0.0).astype(BF)
        low = jnp.where(here, (wanted % 64).astype(F32), 0.0).astype(BF)
        found = nt(marks_bf, high) * 64.0 + nt(marks_bf, low)
        ids_out[:, :, b * 128 : (b + 1) * 128] = (found.astype(I32) - 1).reshape(n, 1, 128)

    pl.semaphore_wait(barrier, n - 1 + nx - 1)

    @pl.loop(0, nz)
    def _(i):
        start_group(lambda q: ids_out.at[pl.ds(q, 1)], lambda q: ids_in.at[pl.ds(q, 1)], group_at(i), 0)

    ids_in[pl.ds(yc, 1)] = ids_out[pl.ds(yc, 1)]
    wait_got(ids_in.at[pl.ds(0, n - 1)], 0)

    def spread(b):
        seen = ids_in[:, :, b * 128 : (b + 1) * 128].reshape(n, 128).astype(F32)
        mine = (iota((n, 128), 0) % PLANE) == (iota((n, 128), 1) // CAP)
        packed = jnp.sum(jnp.where(mine, seen, 0.0).reshape(nz, PLANE, 128), axis=1)
        for g in range(nz):
            row = packed[g : g + 1, :]
            lane_ref[b : b + 1, g * GROUP : (g + 1) * GROUP] = row.astype(I32)
            col_ref[b, g * GROUP : (g + 1) * GROUP, :] = jnp.broadcast_to(row, (128, 128)).T.astype(I32)

    per = 2 if nz % 2 == 0 else 1

    def places(i):
        groups = [group_at(per * i + t) for t in range(per)]
        return groups, [pl.ds(pl.multiple_of(g * GROUP, GROUP), GROUP) for g in groups]

    def ask(b, where):
        wanted = jnp.concatenate([col_ref[b, at, 0:1] for at in where], axis=0)
        pick = one_hot(wanted == iota((per * GROUP, nodes), 1))
        for t in range(per):
            asked_ref[where[t], :] = pick[t * GROUP : (t + 1) * GROUP]
        return pick

    def ask_all(b):
        @pl.loop(0, nz // per)
        def _(i):
            ask(b, places(i)[1])

    def serve(b, t, source):
        @pl.loop(0, nz // per)
        def _(i):
            groups, where = places(i)
            if b == 0 and t == 0:
                pick = ask(b, where)
            else:
                pick = jnp.concatenate([asked_ref[at, :] for at in where], axis=0)
            got = nn(pick, source[:, columns(t)]).astype(BF)
            for k in range(per):
                served[b, where[k], columns(t)] = got[k * GROUP : (k + 1) * GROUP]
            for k in range(per):
                start_group(block(served, b, t), block(answered, b, t), groups[k], 1 + 2 * b + t)

        own_block(served, answered, b, t)

    def prepare(b):
        kv = nn(feat_ref[b], wkv_ref[...]).astype(BF)
        kv_ref[...] = kv
        kvt_ref[...] = kv.T
        datt_ref[...] = nt(cot_ref[b], wo_ref[...]).astype(BF)
        slot_row = slot_ref[b : b + 1, :]
        slot_col = jnp.broadcast_to(slot_row.astype(F32), (128, ends)).T.astype(I32)
        pick_ref[...] = one_hot(slot_col[:, 0:1] == iota((ends, slots), 1))
        pickt_ref[...] = one_hot(iota((slots, ends), 0) == slot_row)
        listed = nidx_ref[b].astype(F32).T
        count = listed.shape[0]
        idx_ref[...] = jnp.where(iota((count, events), 0) < vl_ref[b : b + 1, :], listed, -1.0).astype(I32)
        step = min(64, nbrs)

        @pl.loop(0, nbrs // step)
        def _(k):
            place = iota((step, events), 0) + k * step

            def add(j, total):
                rows = idx_ref[pl.ds(pl.multiple_of(j * 8, 8), 8), :]
                for t in range(8):
                    total = total + jnp.where(place == rows[t : t + 1, :], 1.0, 0.0)
                return total

            mult_ref[pl.ds(pl.multiple_of(k * step, step), step), :] = lax.fori_loop(
                0, count // 8, add, jnp.zeros((step, events), F32)
            )

        since = jnp.broadcast_to(nt_ref[b : b + 1, :].astype(F32), (128, nbrs)).T
        elapsed = jnp.log(1.0 + (et_ref[b : b + 1, :].astype(F32) - since[:, 0:1]))
        mult = mult_ref[...]
        level = jnp.where(mult > 0, jnp.log(jnp.maximum(mult, 1.0)), -1e30)
        for head in range(HEADS):
            bias_ref[head] = level - decay_ref[head] * elapsed
            d = datt_ref[:, pair_columns(head // 2)] * half_lanes(head % 2, 1.0)
            dw_ref[head] = nt(kv_ref[:, pair_columns(head // 2, width)], d)

    half_width = width // HEADS

    def pair_columns(pair, base=0):
        return pl.ds(base + pair * 2 * half_width, 2 * half_width)

    def half_lanes(half, value):
        return jnp.where(iota((1, 2 * half_width), 1) // half_width == half, value, 0.0).astype(BF)

    step = min(512, nodes)

    def name_rows(b):
        @pl.loop(0, nodes // step)
        def _(k):
            at = pl.ds(pl.multiple_of(k * step, step), step)
            marks = jnp.where(iota((step, slots), 0) + k * step == lane_ref[b : b + 1, :], 1.0, 0.0)
            counts = jnp.sum(marks, axis=1, keepdims=True)
            named_ref[at, :] = marks.astype(BF)
            inverse = jnp.where(counts > 0, 1.0 / jnp.maximum(counts, 1.0), 0.0)
            inverse_ref[at, :] = jnp.broadcast_to(inverse, (step, 128))

    def fetch(b):
        for t in range(2):
            wait_got(others(answered, b, t), 1 + 2 * b + t)
            got = nn(pick_ref[...], answered[b, :, columns(t)]).astype(BF)
            rows_ref[b, 0, :, columns(t)] = got[:events]
            rows_ref[b, 1, :, columns(t)] = got[events:]

    def update(b, t):
        @pl.loop(0, 2)
        def _(k):
            state = rows_ref[b, k]
            partner = rows_ref[b, 1 - k]
            gate = [slice(i * width + t * wide, i * width + (t + 1) * wide) for i in range(3)]
            reset = sigmoid(nn(partner, gi_ref[:, gate[0]]) + nn(state, gh_ref[:, gate[0]]))
            keep = sigmoid(nn(partner, gi_ref[:, gate[1]]) + nn(state, gh_ref[:, gate[1]]))
            candidate = jnp.tanh(nn(partner, gi_ref[:, gate[2]]) + reset * nn(state, gh_ref[:, gate[2]]))
            old = rows_ref[b, k, :, columns(t)].astype(F32)
            upd_ref[pl.ds(pl.multiple_of(k * events, events), events), columns(t)] = (
                candidate + keep * (old - candidate)
            ).astype(BF)

        @pl.loop(0, nz // per)
        def _(i):
            groups, where = places(i)
            pick = jnp.concatenate([pickt_ref[at, :] for at in where], axis=0)
            got = nn(pick, upd_ref[:, columns(t)]).astype(BF)
            for k in range(per):
                outgoing[b, where[k], columns(t)] = got[k * GROUP : (k + 1) * GROUP]
            for k in range(per):
                start_group(block(outgoing, b, t), block(arrived, b, t), groups[k], 5 + 2 * b + t)

        own_block(outgoing, arrived, b, t)

    def apply(b, t, source, target, store=None):
        wait_got(others(arrived, b, t), 5 + 2 * b + t)

        @pl.loop(0, nodes // step)
        def _(k):
            at = pl.ds(pl.multiple_of(k * step, step), step)
            sums = nn(named_ref[at, :], arrived[b, :, columns(t)])
            inverse = inverse_ref[at, 0:1]
            old = source[at, columns(t)].astype(F32)
            target[at, columns(t)] = jnp.where(inverse > 0, sums * inverse, old).astype(BF)
            if store:
                store(k).start()

    def store_memory(k):
        at = pl.ds(pl.multiple_of(k * step, step), step)
        return pltpu.make_async_copy(newmem_ref.at[at], newmem_hbm.at[at], out_sem.at[2 + k])

    def store_embeddings(b):
        return pltpu.make_async_copy(emb_ref.at[b], emb_hbm.at[b], out_sem.at[b])

    scale = 1.0 / math.sqrt(half_width)

    def head_query(head):
        return q_ref[:, pair_columns(head // 2)] * half_lanes(head % 2, scale)

    def head_rows(head, base=0):
        return pl.ds(base + head * half_width, half_width)

    def add_grad(b, ref, cols, grad):
        ref[:, cols] = grad if b == 0 else ref[:, cols] + grad

    def attend(b):
        q_ref[...] = nn(rows_ref[b, 0], wq_ref[...]).astype(BF)

        def score(head):
            return nt(kv_ref[:, pair_columns(head // 2)], head_query(head)) + bias_ref[head]

        def weigh(head, logits):
            weighted = jnp.exp(logits - jnp.max(logits, axis=0, keepdims=True))
            weights = weighted * (1.0 / jnp.sum(weighted, axis=0, keepdims=True))
            bias_ref[head] = weights
            return weights.astype(BF)

        def combine(head, w, held):
            att_ref[head_rows(head), :] = nn(kvt_ref[head_rows(head, width), :], w).astype(BF)
            d = datt_ref[:, pair_columns(head // 2)] * half_lanes(head % 2, 1.0)
            dv = nn(w, d)
            if head % 2 == 0:
                return dv
            dkv_ref[:, pair_columns(head // 2, width)] = (held + dv).astype(BF)

        logits = score(0)
        ready = held = None
        for head in range(HEADS):
            ahead = score(head + 1) if head + 1 < HEADS else None
            if head:
                held = combine(head - 1, ready, held)
            ready = weigh(head, logits)
            logits = ahead
        combine(HEADS - 1, ready, held)
        values = pl.ds(width, width)
        add_grad(b, ga_ref, values, nn(att_ref[...], cot_ref[b]))
        add_grad(b, gb_ref, values, nn(feat_ref[b].T, dkv_ref[:, values]))

    def attend_back(b):
        def weigh(head):
            weights = bias_ref[head]
            dw = dw_ref[head]
            inner = jnp.sum(dw * weights, axis=0, keepdims=True)
            return (weights * (dw - inner)).astype(BF)

        def combine(head, dl, held):
            dq_ref[head_rows(head), :] = (nn(kvt_ref[head_rows(head), :], dl) * scale).astype(BF)
            dk = nn(dl, head_query(head))
            if head % 2 == 0:
                return dk
            dkv_ref[:, pair_columns(head // 2)] = (held + dk).astype(BF)

        ready = held = None
        for head in range(HEADS):
            if head:
                held = combine(head - 1, ready, held)
            ready = weigh(head)
        combine(HEADS - 1, ready, held)
        keys = pl.ds(0, width)
        add_grad(b, ga_ref, keys, nn(rows_ref[b, 0].T, dq_ref[...].T))
        add_grad(b, gb_ref, keys, nn(feat_ref[b].T, dkv_ref[:, keys]))

    def embed(b):
        source = rows_ref[b, 0].astype(F32)
        emb_ref[b] = (source + nn(att_ref[...].T, wo_ref[...])).astype(BF)
        store_embeddings(b).start()

    part = 2 * width // n
    plane = nz * part
    cut = width // nx

    def copy_to(src, dst, where, sem):
        pltpu.make_async_remote_copy(
            src_ref=src,
            dst_ref=dst,
            send_sem=send_sem.at[sem],
            recv_sem=recv_sem.at[sem],
            device_id=where,
            device_id_type=MESH,
        ).start()

    def rows_of_y(k):
        return pl.ds(pl.multiple_of(k * plane, plane), plane)

    def rows_of_z(k):
        return pl.ds(pl.multiple_of(k * part, part), part)

    def reduce_core(t):
        share = part // 2

        @pl.loop(0, nz)
        def _(zz):
            cols = pl.ds(t * width, width)
            for j in range(PLANE):
                rows = pl.ds(pl.multiple_of((zz * PLANE + j) * share, share), share)
                both = jnp.concatenate([ga_ref[rows, cols], gb_ref[rows, cols]], axis=0).astype(BF)
                at = pl.ds(pl.multiple_of((j // 2 * nz + zz) * part, part), part)
                for k in range(nx):
                    h1[t, j % 2, k, at, :] = both[:, k * cut : (k + 1) * cut]

        copy_to(h1.at[t, 1 - c], r1.at[t], {"mem": me + 1 - 2 * c}, 9 + t)

    def reduce_x(t):
        wait_got(r1.at[t], 9 + t)
        for k in range(nx):
            h2[t, k] = (h1[t, c, k].astype(F32) + r1[t, k].astype(F32)).astype(BF)
        for k in range(1, nx):
            xx = (x + k) % nx
            copy_to(h2.at[t, xx], r2.at[t, k - 1], {"rep": xx}, 11 + t)

    def reduce_y(t):
        total = h2[t, x].astype(F32)
        if nx > 1:
            wait_got(r2.at[t], 11 + t)
            for k in range(nx - 1):
                total = total + r2[t, k].astype(F32)
        h3[t] = total.astype(BF)
        for k in range(1, NY):
            yy = (y + k) % NY
            copy_to(h3.at[t, rows_of_y(yy)], r3.at[t, k - 1], {"mem": z * PLANE + yy * 2 + c}, 13 + t)

    def reduce_z():
        for t in range(2):
            wait_got(r3.at[t], 13 + t)
            total = h3[t, rows_of_y(y), :].astype(F32)
            for k in range(NY - 1):
                total = total + r3[t, k].astype(F32)
            h4[:, t * cut : (t + 1) * cut] = total.astype(BF)
        for k in range(1, nz):
            zz = lax.rem(z + k, nz)
            copy_to(h4.at[rows_of_z(zz)], r4.at[k - 1], {"mem": zz * PLANE + yc}, 15)

    def share_x():
        total = h4[rows_of_z(z), :].astype(F32)
        if nz > 1:
            wait_got(r4, 15)
            for k in range(nz - 1):
                total = total + r4[k].astype(F32)
        fin[x] = total
        for k in range(1, nx):
            copy_to(fin.at[x], fin.at[x], {"rep": lax.rem(x + k, nx)}, 16)

    def finish():
        if nx > 1:
            wait_got(fin.at[pl.ds(0, nx - 1)], 16)
        share = part // 2
        for k in range(nx):
            total = fin[k]
            at = slice(k * cut, (k + 1) * cut)
            gq_ref[:, at] = total[:share, :cut]
            go_ref[:, at] = total[:share, cut:]
            gkv_ref[:, at] = total[share:, :cut]
            gkv_ref[:, width + k * cut : width + (k + 1) * cut] = total[share:, cut:]

    spread(0)
    loaded("mem")
    serve(0, 0, mem_ref)
    serve(0, 1, mem_ref)
    spread(1)
    loaded("nidx", "feat", "wkv", "wo", "cot")
    prepare(0)
    name_rows(0)
    ask_all(1)
    loaded("gi", "gh", "wq")
    fetch(0)
    update(0, 0)
    update(0, 1)
    attend(0)
    attend_back(0)
    embed(0)
    for t in range(2):
        apply(0, t, mem_ref, mem1)
        serve(1, t, mem1)
    prepare(1)
    name_rows(1)
    fetch(1)
    update(1, 0)
    attend(1)
    reduce_core(1)
    attend_back(1)
    reduce_x(1)
    reduce_core(0)
    update(1, 1)
    reduce_x(0)
    embed(1)
    apply(1, 0, mem1, newmem_ref)
    reduce_y(1)
    reduce_y(0)
    reduce_z()
    apply(1, 1, mem1, newmem_ref, store_memory)
    share_x()
    finish()

    for b in range(2):
        for t in range(2):
            wait_sent(others(served, b, t), 1 + 2 * b + t)
            wait_sent(others(outgoing, b, t), 5 + 2 * b + t)
        store_embeddings(b).wait()
    wait_sent(ids_out.at[pl.ds(0, n - 1)], 0)
    for t in range(2):
        wait_sent(r1.at[t], 9 + t)
        if nx > 1:
            wait_sent(r2.at[t], 11 + t)
        wait_sent(r3.at[t], 13 + t)
    if nz > 1:
        wait_sent(r4, 15)
    if nx > 1:
        wait_sent(fin.at[pl.ds(0, nx - 1)], 16)
    for k in range(nodes // step):
        store_memory(k).wait()


def hand_on(*refs):
    count = (len(refs) - 1) // 3
    sem = refs[-1]
    steps = []
    for src, dst, held in zip(refs[:count], refs[count : 2 * count], refs[2 * count : 3 * count]):
        rows = src.shape[0]
        pieces = 8 if rows % 128 == 0 else 1
        for k in range(pieces):
            at = pl.ds(k * (rows // pieces), rows // pieces)
            get = pltpu.make_async_copy(src.at[at], held.at[at], sem.at[0, len(steps)])
            put = pltpu.make_async_copy(held.at[at], dst.at[at], sem.at[1, len(steps)])
            get.start()
            steps.append((get, put))
    for get, put in steps:
        get.wait()
        put.start()
    for _, put in steps:
        put.wait()


def on_device(
    memory,
    endpoint_owner,
    endpoint_row,
    event_time,
    neighbour_time,
    neighbour_feat,
    neighbour_index,
    valid_length,
    decay_rate,
    w_query,
    w_keyval,
    w_out,
    gru_input,
    gru_hidden,
    cotangent,
):
    n = lax.axis_size("mem")
    nx = lax.axis_size("rep")
    nz = n // PLANE
    _, nodes, width = memory.shape
    batches, events = event_time.shape[1:]
    nbrs = neighbour_time.shape[2]
    listed = neighbour_index.shape[3]
    ends = 2 * events
    slots = n * CAP
    part = 2 * width // n
    plane = nz * part
    half = n // 2 * part
    cut = width // nx
    owner = endpoint_owner[0].transpose(0, 2, 1)
    row = endpoint_row[0].transpose(0, 2, 1)
    vmem = pl.BlockSpec(memory_space=pltpu.VMEM)
    shape = jax.ShapeDtypeStruct
    share = width // n
    hbm = pl.BlockSpec(memory_space=pl.ANY)
    outputs = (
        shape((nodes, width), BF),
        shape((batches, events, width), BF),
        shape((share, width), F32),
        shape((share, 2 * width), F32),
        shape((share, width), F32),
    )
    results = pl.pallas_call(
        functools.partial(window, nx),
        out_shape=outputs,
        in_specs=[vmem] * 5 + [pl.BlockSpec(memory_space=pltpu.SMEM)] + [hbm] * 9,
        out_specs=(hbm,) * 2 + (vmem,) * 3,
        scratch_shapes=[
            pltpu.VMEM((batches, events, listed), I32),
            pltpu.VMEM((nodes, width), BF),
            pltpu.VMEM((batches, nbrs, width), BF),
            pltpu.VMEM((batches, events, width), BF),
            pltpu.VMEM((width, width), BF),
            pltpu.VMEM((width, 2 * width), BF),
            pltpu.VMEM((width, width), BF),
            pltpu.VMEM((width, 3 * width), BF),
            pltpu.VMEM((width, 3 * width), BF),
            pltpu.VMEM((nodes, width), BF),
            pltpu.VMEM((batches, events, width), BF),
            pltpu.SemaphoreType.DMA((9,)),
            pltpu.SemaphoreType.DMA((2 + nodes // min(512, nodes),)),
            pltpu.VMEM((n, 1, 256), I32),
            pltpu.VMEM((n, 1, 256), I32),
            pltpu.VMEM((batches, slots, width), BF),
            pltpu.VMEM((batches, slots, width), BF),
            pltpu.VMEM((batches, slots, width), BF),
            pltpu.VMEM((batches, slots, width), BF),
            pltpu.VMEM((nodes, width), BF),
            pltpu.VMEM((8, ends), I32),
            pltpu.VMEM((8, slots), I32),
            pltpu.VMEM((batches, slots, 128), I32),
            pltpu.VMEM((ends, slots), BF),
            pltpu.VMEM((slots, ends), BF),
            pltpu.VMEM((slots, nodes), BF),
            pltpu.VMEM((nodes, slots), BF),
            pltpu.VMEM((nodes, 128), F32),
            pltpu.VMEM((batches, 2, events, width), BF),
            pltpu.VMEM((ends, width), BF),
            pltpu.VMEM((listed, events), I32),
            pltpu.VMEM((nbrs, events), F32),
            pltpu.VMEM((HEADS, nbrs, events), F32),
            pltpu.VMEM((HEADS, nbrs, events), F32),
            pltpu.VMEM((nbrs, 2 * width), BF),
            pltpu.VMEM((2 * width, nbrs), BF),
            pltpu.VMEM((events, width), BF),
            pltpu.VMEM((events, width), BF),
            pltpu.VMEM((width, events), BF),
            pltpu.VMEM((width, events), BF),
            pltpu.VMEM((nbrs, 2 * width), BF),
            pltpu.VMEM((width, 2 * width), F32),
            pltpu.VMEM((width, 2 * width), F32),
            pltpu.VMEM((2, 2, nx, half, cut), BF),
            pltpu.VMEM((2, nx, half, cut), BF),
            pltpu.VMEM((2, nx, half, cut), BF),
            pltpu.VMEM((2, max(nx - 1, 1), half, cut), BF),
            pltpu.VMEM((2, half, cut), BF),
            pltpu.VMEM((2, NY - 1, plane, cut), BF),
            pltpu.VMEM((plane, 2 * cut), BF),
            pltpu.VMEM((max(nz - 1, 1), part, 2 * cut), BF),
            pltpu.VMEM((nx, part, 2 * cut), F32),
            pltpu.SemaphoreType.DMA((17,)),
            pltpu.SemaphoreType.DMA((17,)),
        ],
        compiler_params=pltpu.CompilerParams(
            collective_id=0, has_side_effects=True, vmem_limit_bytes=60 * 1024 * 1024
        ),
        name="window",
    )(
        owner,
        row,
        event_time[0],
        neighbour_time[0],
        valid_length[0],
        decay_rate,
        neighbour_index[0],
        memory[0],
        neighbour_feat[0],
        cotangent[0],
        w_query,
        w_keyval,
        w_out,
        gru_input,
        gru_hidden,
    )
    new_memory, embeddings, gq, gkv, go = pl.pallas_call(
        hand_on,
        out_shape=outputs,
        in_specs=[hbm] * 5,
        out_specs=(hbm,) * 5,
        scratch_shapes=[pltpu.VMEM(out.shape, out.dtype) for out in outputs] + [pltpu.SemaphoreType.DMA((2, 16))],
        compiler_params=pltpu.CompilerParams(vmem_limit_bytes=60 * 1024 * 1024),
        name="hand_on",
    )(*results)
    return (new_memory[None], embeddings[None], gq, gkv, go)


def solution(mesh):
    return jax.shard_map(
        on_device,
        mesh=mesh,
        in_specs=(
            P("rep", "mem", None),
            P("rep", None, "mem", None),
            P("rep", None, "mem", None),
            P("rep", None, "mem"),
            P("rep", None, "mem"),
            P("rep", None, "mem", None),
            P("rep", None, "mem", None),
            P("rep", None, "mem"),
            P(),
            P(),
            P(),
            P(),
            P(),
            P(),
            P("rep", None, "mem", None),
        ),
        out_specs=(
            P("rep", "mem", None),
            P("rep", None, "mem", None),
            P("mem", None),
            P("mem", None),
            P("mem", None),
        ),
        check_vma=False,
    )
```

```python
import functools
import math

import jax
import jax.numpy as jnp
from jax import lax
from jax.experimental import pallas as pl
from jax.experimental.pallas import tpu as pltpu
from jax.sharding import PartitionSpec as P

MESH = pl.DeviceIdType.MESH
BF = jnp.bfloat16
F32 = jnp.float32
I32 = jnp.int32
CAP = 16
PLANE = 8
GROUP = CAP * PLANE
HEADS = 8
NY = 4


def nn(a, b):
    return lax.dot_general(a, b, (((1,), (0,)), ((), ())), preferred_element_type=F32)


def nt(a, b):
    return lax.dot_general(a, b, (((1,), (1,)), ((), ())), preferred_element_type=F32)


def sigmoid(a):
    return 0.5 * jnp.tanh(0.5 * a) + 0.5


def iota(shape, axis):
    return lax.broadcasted_iota(I32, shape, axis)


def one_hot(mask):
    return jnp.where(mask, 1.0, 0.0).astype(BF)


def window(
    nx,
    owner_ref,
    row_ref,
    et_ref,
    nt_ref,
    vl_ref,
    decay_ref,
    nidx_hbm,
    mem_hbm,
    feat_hbm,
    cot_hbm,
    wq_hbm,
    wkv_hbm,
    wo_hbm,
    gi_hbm,
    gh_hbm,
    newmem_hbm,
    emb_hbm,
    gq_ref,
    gkv_ref,
    go_ref,
    nidx_ref,
    mem_ref,
    feat_ref,
    cot_ref,
    wq_ref,
    wkv_ref,
    wo_ref,
    gi_ref,
    gh_ref,
    newmem_ref,
    emb_ref,
    in_sem,
    out_sem,
    ids_out,
    ids_in,
    served,
    answered,
    outgoing,
    arrived,
    mem1,
    slot_ref,
    lane_ref,
    col_ref,
    pick_ref,
    pickt_ref,
    asked_ref,
    named_ref,
    inverse_ref,
    rows_ref,
    upd_ref,
    idx_ref,
    mult_ref,
    bias_ref,
    dw_ref,
    kv_ref,
    kvt_ref,
    q_ref,
    datt_ref,
    att_ref,
    dq_ref,
    dkv_ref,
    ga_ref,
    gb_ref,
    h1,
    r1,
    h2,
    r2,
    h3,
    r3,
    h4,
    r4,
    fin,
    send_sem,
    recv_sem,
):
    n = ids_in.shape[0]
    nz = n // PLANE
    nodes, width = mem_ref.shape
    events = et_ref.shape[1]
    nbrs = nt_ref.shape[1]
    ends = 2 * events
    slots = n * CAP
    wide = width // 2
    me = lax.axis_index("mem")
    x = lax.axis_index("rep")
    z = lax.div(me, PLANE)
    yc = lax.rem(me, PLANE)
    y = lax.div(yc, 2)
    c = lax.rem(yc, 2)

    loads = {}
    for at, (name, src, dst) in enumerate(
        (
            ("mem", mem_hbm, mem_ref),
            ("nidx", nidx_hbm, nidx_ref),
            ("feat", feat_hbm, feat_ref),
            ("wkv", wkv_hbm, wkv_ref),
            ("gi", gi_hbm, gi_ref),
            ("gh", gh_hbm, gh_ref),
            ("wq", wq_hbm, wq_ref),
            ("wo", wo_hbm, wo_ref),
            ("cot", cot_hbm, cot_ref),
        )
    ):
        loads[name] = pltpu.make_async_copy(src, dst, in_sem.at[at])
        loads[name].start()

    def loaded(*names):
        for name in names:
            loads[name].wait()

    barrier = pltpu.get_barrier_semaphore()

    @pl.loop(1, n)
    def _(k):
        pl.semaphore_signal(barrier, inc=1, device_id={"mem": lax.rem(me + k, n)}, device_id_type=MESH)

    for k in range(1, nx):
        pl.semaphore_signal(barrier, inc=1, device_id={"rep": (x + k) % nx}, device_id_type=MESH)

    def group_at(i):
        h = lax.div(i + 1, 2)
        return nz // 2 + h * (1 - 2 * lax.rem(i, 2))

    def start_group(src, dst, g, sem):
        there = lax.rem(g + z, nz) * PLANE
        mine = lax.rem(nz - g, nz) * PLANE + yc
        for j in range(PLANE):
            turned = lax.rem(yc + j, PLANE)

            def send(turned=turned):
                pltpu.make_async_remote_copy(
                    src_ref=src(g * PLANE + turned),
                    dst_ref=dst(mine),
                    send_sem=send_sem.at[sem],
                    recv_sem=recv_sem.at[sem],
                    device_id={"mem": there + turned},
                    device_id_type=MESH,
                ).start()

            if j:
                send()
            else:
                pl.when(g > 0)(send)

    def columns(t):
        return pl.ds(t * wide, wide)

    def block(ref, b, t):
        return lambda q: ref.at[b, pl.ds(pl.multiple_of(q * CAP, CAP), CAP), columns(t)]

    def own_block(src, dst, b, t):
        here = pl.ds(pl.multiple_of(yc * CAP, CAP), CAP)
        dst[b, here, columns(t)] = src[b, here, columns(t)]

    def others(ref, b, t):
        return ref.at[b, pl.ds(0, slots - CAP), columns(t)]

    def wait_sent(view, sem):
        pltpu.make_async_copy(view, view, send_sem.at[sem]).wait()

    def wait_got(view, sem):
        pltpu.make_async_copy(view, view, recv_sem.at[sem]).wait()

    before = one_hot(iota((ends, ends), 0) < iota((ends, ends), 1))
    for b in range(2):
        own = jnp.concatenate([owner_ref[b, 0:1, :], owner_ref[b, 1:2, :]], axis=1) - z * PLANE
        own = jnp.where(own < 0, own + n, own)
        marks = jnp.where(iota((n, ends), 0) == own, 1.0, 0.0)
        marks_bf = marks.astype(BF)
        rank = jnp.sum(nn(marks_bf, before) * marks, axis=0, keepdims=True).astype(I32)
        slot_ref[b : b + 1, :] = own * CAP + rank
        wanted = jnp.concatenate([row_ref[b, 0:1, :], row_ref[b, 1:2, :]], axis=1) + 1
        here = (iota((128, ends), 0) % CAP) == rank
        high = jnp.where(here, (wanted // 64).astype(F32), 0.0).astype(BF)
        low = jnp.where(here, (wanted % 64).astype(F32), 0.0).astype(BF)
        found = nt(marks_bf, high) * 64.0 + nt(marks_bf, low)
        ids_out[:, :, b * 128 : (b + 1) * 128] = (found.astype(I32) - 1).reshape(n, 1, 128)

    pl.semaphore_wait(barrier, n - 1 + nx - 1)

    @pl.loop(0, nz)
    def _(i):
        start_group(lambda q: ids_out.at[pl.ds(q, 1)], lambda q: ids_in.at[pl.ds(q, 1)], group_at(i), 0)

    ids_in[pl.ds(yc, 1)] = ids_out[pl.ds(yc, 1)]
    wait_got(ids_in.at[pl.ds(0, n - 1)], 0)

    def spread(b):
        seen = ids_in[:, :, b * 128 : (b + 1) * 128].reshape(n, 128).astype(F32)
        mine = (iota((n, 128), 0) % PLANE) == (iota((n, 128), 1) // CAP)
        packed = jnp.sum(jnp.where(mine, seen, 0.0).reshape(nz, PLANE, 128), axis=1)
        for g in range(nz):
            row = packed[g : g + 1, :]
            lane_ref[b : b + 1, g * GROUP : (g + 1) * GROUP] = row.astype(I32)
            col_ref[b, g * GROUP : (g + 1) * GROUP, :] = jnp.broadcast_to(row, (128, 128)).T.astype(I32)

    per = 2 if nz % 2 == 0 else 1

    def places(i):
        groups = [group_at(per * i + t) for t in range(per)]
        return groups, [pl.ds(pl.multiple_of(g * GROUP, GROUP), GROUP) for g in groups]

    def ask(b, where):
        wanted = jnp.concatenate([col_ref[b, at, 0:1] for at in where], axis=0)
        pick = one_hot(wanted == iota((per * GROUP, nodes), 1))
        for t in range(per):
            asked_ref[where[t], :] = pick[t * GROUP : (t + 1) * GROUP]
        return pick

    def ask_all(b):
        @pl.loop(0, nz // per)
        def _(i):
            ask(b, places(i)[1])

    def serve(b, t, source):
        @pl.loop(0, nz // per)
        def _(i):
            groups, where = places(i)
            if b == 0 and t == 0:
                pick = ask(b, where)
            else:
                pick = jnp.concatenate([asked_ref[at, :] for at in where], axis=0)
            got = nn(pick, source[:, columns(t)]).astype(BF)
            for k in range(per):
                served[b, where[k], columns(t)] = got[k * GROUP : (k + 1) * GROUP]
            for k in range(per):
                start_group(block(served, b, t), block(answered, b, t), groups[k], 1 + 2 * b + t)

        own_block(served, answered, b, t)

    def prepare(b):
        kv = nn(feat_ref[b], wkv_ref[...]).astype(BF)
        kv_ref[...] = kv
        kvt_ref[...] = kv.T
        datt_ref[...] = nt(cot_ref[b], wo_ref[...]).astype(BF)
        slot_row = slot_ref[b : b + 1, :]
        slot_col = jnp.broadcast_to(slot_row.astype(F32), (128, ends)).T.astype(I32)
        pick_ref[...] = one_hot(slot_col[:, 0:1] == iota((ends, slots), 1))
        pickt_ref[...] = one_hot(iota((slots, ends), 0) == slot_row)
        listed = nidx_ref[b].astype(F32).T
        count = listed.shape[0]
        idx_ref[...] = jnp.where(iota((count, events), 0) < vl_ref[b : b + 1, :], listed, -1.0).astype(I32)
        step = min(64, nbrs)

        @pl.loop(0, nbrs // step)
        def _(k):
            place = iota((step, events), 0) + k * step

            def add(j, total):
                rows = idx_ref[pl.ds(pl.multiple_of(j * 8, 8), 8), :]
                for t in range(8):
                    total = total + jnp.where(place == rows[t : t + 1, :], 1.0, 0.0)
                return total

            mult_ref[pl.ds(pl.multiple_of(k * step, step), step), :] = lax.fori_loop(
                0, count // 8, add, jnp.zeros((step, events), F32)
            )

        since = jnp.broadcast_to(nt_ref[b : b + 1, :].astype(F32), (128, nbrs)).T
        elapsed = jnp.log(1.0 + (et_ref[b : b + 1, :].astype(F32) - since[:, 0:1]))
        mult = mult_ref[...]
        level = jnp.where(mult > 0, jnp.log(jnp.maximum(mult, 1.0)), -1e30)
        for head in range(HEADS):
            bias_ref[head] = level - decay_ref[head] * elapsed
            d = datt_ref[:, pair_columns(head // 2)] * half_lanes(head % 2, 1.0)
            dw_ref[head] = nt(kv_ref[:, pair_columns(head // 2, width)], d)

    half_width = width // HEADS

    def pair_columns(pair, base=0):
        return pl.ds(base + pair * 2 * half_width, 2 * half_width)

    def half_lanes(half, value):
        return jnp.where(iota((1, 2 * half_width), 1) // half_width == half, value, 0.0).astype(BF)

    step = min(512, nodes)

    def name_rows(b):
        @pl.loop(0, nodes // step)
        def _(k):
            at = pl.ds(pl.multiple_of(k * step, step), step)
            marks = jnp.where(iota((step, slots), 0) + k * step == lane_ref[b : b + 1, :], 1.0, 0.0)
            counts = jnp.sum(marks, axis=1, keepdims=True)
            named_ref[at, :] = marks.astype(BF)
            inverse = jnp.where(counts > 0, 1.0 / jnp.maximum(counts, 1.0), 0.0)
            inverse_ref[at, :] = jnp.broadcast_to(inverse, (step, 128))

    def fetch(b):
        for t in range(2):
            wait_got(others(answered, b, t), 1 + 2 * b + t)
            got = nn(pick_ref[...], answered[b, :, columns(t)]).astype(BF)
            rows_ref[b, 0, :, columns(t)] = got[:events]
            rows_ref[b, 1, :, columns(t)] = got[events:]

    def update(b, t):
        @pl.loop(0, 2)
        def _(k):
            state = rows_ref[b, k]
            partner = rows_ref[b, 1 - k]
            gate = [slice(i * width + t * wide, i * width + (t + 1) * wide) for i in range(3)]
            reset = sigmoid(nn(partner, gi_ref[:, gate[0]]) + nn(state, gh_ref[:, gate[0]]))
            keep = sigmoid(nn(partner, gi_ref[:, gate[1]]) + nn(state, gh_ref[:, gate[1]]))
            candidate = jnp.tanh(nn(partner, gi_ref[:, gate[2]]) + reset * nn(state, gh_ref[:, gate[2]]))
            old = rows_ref[b, k, :, columns(t)].astype(F32)
            upd_ref[pl.ds(pl.multiple_of(k * events, events), events), columns(t)] = (
                candidate + keep * (old - candidate)
            ).astype(BF)

        @pl.loop(0, nz // per)
        def _(i):
            groups, where = places(i)
            pick = jnp.concatenate([pickt_ref[at, :] for at in where], axis=0)
            got = nn(pick, upd_ref[:, columns(t)]).astype(BF)
            for k in range(per):
                outgoing[b, where[k], columns(t)] = got[k * GROUP : (k + 1) * GROUP]
            for k in range(per):
                start_group(block(outgoing, b, t), block(arrived, b, t), groups[k], 5 + 2 * b + t)

        own_block(outgoing, arrived, b, t)

    def apply(b, t, source, target, store=None):
        wait_got(others(arrived, b, t), 5 + 2 * b + t)

        @pl.loop(0, nodes // step)
        def _(k):
            at = pl.ds(pl.multiple_of(k * step, step), step)
            sums = nn(named_ref[at, :], arrived[b, :, columns(t)])
            inverse = inverse_ref[at, 0:1]
            old = source[at, columns(t)].astype(F32)
            target[at, columns(t)] = jnp.where(inverse > 0, sums * inverse, old).astype(BF)
            if store:
                store(k).start()

    def store_memory(k):
        at = pl.ds(pl.multiple_of(k * step, step), step)
        return pltpu.make_async_copy(newmem_ref.at[at], newmem_hbm.at[at], out_sem.at[2 + k])

    def store_embeddings(b):
        return pltpu.make_async_copy(emb_ref.at[b], emb_hbm.at[b], out_sem.at[b])

    scale = 1.0 / math.sqrt(half_width)

    def head_query(head):
        return q_ref[:, pair_columns(head // 2)] * half_lanes(head % 2, scale)

    def head_rows(head, base=0):
        return pl.ds(base + head * half_width, half_width)

    def add_grad(b, ref, cols, grad):
        ref[:, cols] = grad if b == 0 else ref[:, cols] + grad

    def attend(b):
        q_ref[...] = nn(rows_ref[b, 0], wq_ref[...]).astype(BF)

        def score(head):
            return nt(kv_ref[:, pair_columns(head // 2)], head_query(head)) + bias_ref[head]

        def weigh(head, logits):
            weighted = jnp.exp(logits - jnp.max(logits, axis=0, keepdims=True))
            weights = weighted * (1.0 / jnp.sum(weighted, axis=0, keepdims=True))
            bias_ref[head] = weights
            return weights.astype(BF)

        def combine(head, w, held):
            att_ref[head_rows(head), :] = nn(kvt_ref[head_rows(head, width), :], w).astype(BF)
            d = datt_ref[:, pair_columns(head // 2)] * half_lanes(head % 2, 1.0)
            dv = nn(w, d)
            if head % 2 == 0:
                return dv
            dkv_ref[:, pair_columns(head // 2, width)] = (held + dv).astype(BF)

        logits = score(0)
        ready = held = None
        for head in range(HEADS):
            ahead = score(head + 1) if head + 1 < HEADS else None
            if head:
                held = combine(head - 1, ready, held)
            ready = weigh(head, logits)
            logits = ahead
        combine(HEADS - 1, ready, held)
        values = pl.ds(width, width)
        add_grad(b, ga_ref, values, nn(att_ref[...], cot_ref[b]))
        add_grad(b, gb_ref, values, nn(feat_ref[b].T, dkv_ref[:, values]))

    def attend_back(b):
        def weigh(head):
            weights = bias_ref[head]
            dw = dw_ref[head]
            inner = jnp.sum(dw * weights, axis=0, keepdims=True)
            return (weights * (dw - inner)).astype(BF)

        def combine(head, dl, held):
            dq_ref[head_rows(head), :] = (nn(kvt_ref[head_rows(head), :], dl) * scale).astype(BF)
            dk = nn(dl, head_query(head))
            if head % 2 == 0:
                return dk
            dkv_ref[:, pair_columns(head // 2)] = (held + dk).astype(BF)

        ready = held = None
        for head in range(HEADS):
            if head:
                held = combine(head - 1, ready, held)
            ready = weigh(head)
        combine(HEADS - 1, ready, held)
        keys = pl.ds(0, width)
        add_grad(b, ga_ref, keys, nn(rows_ref[b, 0].T, dq_ref[...].T))
        add_grad(b, gb_ref, keys, nn(feat_ref[b].T, dkv_ref[:, keys]))

    def embed(b):
        source = rows_ref[b, 0].astype(F32)
        emb_ref[b] = (source + nn(att_ref[...].T, wo_ref[...])).astype(BF)
        store_embeddings(b).start()

    part = 2 * width // n
    plane = nz * part
    cut = width // nx

    def copy_to(src, dst, where, sem):
        pltpu.make_async_remote_copy(
            src_ref=src,
            dst_ref=dst,
            send_sem=send_sem.at[sem],
            recv_sem=recv_sem.at[sem],
            device_id=where,
            device_id_type=MESH,
        ).start()

    def rows_of_y(k):
        return pl.ds(pl.multiple_of(k * plane, plane), plane)

    def rows_of_z(k):
        return pl.ds(pl.multiple_of(k * part, part), part)

    def reduce_core(t):
        share = part // 2

        @pl.loop(0, nz)
        def _(zz):
            cols = pl.ds(t * width, width)
            for j in range(PLANE):
                rows = pl.ds(pl.multiple_of((zz * PLANE + j) * share, share), share)
                both = jnp.concatenate([ga_ref[rows, cols], gb_ref[rows, cols]], axis=0).astype(BF)
                at = pl.ds(pl.multiple_of((j // 2 * nz + zz) * part, part), part)
                for k in range(nx):
                    h1[t, j % 2, k, at, :] = both[:, k * cut : (k + 1) * cut]

        copy_to(h1.at[t, 1 - c], r1.at[t], {"mem": me + 1 - 2 * c}, 9 + t)

    def reduce_x(t):
        wait_got(r1.at[t], 9 + t)
        for k in range(nx):
            h2[t, k] = (h1[t, c, k].astype(F32) + r1[t, k].astype(F32)).astype(BF)
        for k in range(1, nx):
            xx = (x + k) % nx
            copy_to(h2.at[t, xx], r2.at[t, k - 1], {"rep": xx}, 11 + t)

    def reduce_y(t):
        total = h2[t, x].astype(F32)
        if nx > 1:
            wait_got(r2.at[t], 11 + t)
            for k in range(nx - 1):
                total = total + r2[t, k].astype(F32)
        h3[t] = total.astype(BF)
        for k in range(1, NY):
            yy = (y + k) % NY
            copy_to(h3.at[t, rows_of_y(yy)], r3.at[t, k - 1], {"mem": z * PLANE + yy * 2 + c}, 13 + t)

    def reduce_z():
        for t in range(2):
            wait_got(r3.at[t], 13 + t)
            total = h3[t, rows_of_y(y), :].astype(F32)
            for k in range(NY - 1):
                total = total + r3[t, k].astype(F32)
            h4[:, t * cut : (t + 1) * cut] = total.astype(BF)
        for k in range(1, nz):
            zz = lax.rem(z + k, nz)
            copy_to(h4.at[rows_of_z(zz)], r4.at[k - 1], {"mem": zz * PLANE + yc}, 15)

    def share_x():
        total = h4[rows_of_z(z), :].astype(F32)
        if nz > 1:
            wait_got(r4, 15)
            for k in range(nz - 1):
                total = total + r4[k].astype(F32)
        fin[x] = total
        for k in range(1, nx):
            copy_to(fin.at[x], fin.at[x], {"rep": lax.rem(x + k, nx)}, 16)

    def finish():
        if nx > 1:
            wait_got(fin.at[pl.ds(0, nx - 1)], 16)
        share = part // 2
        for k in range(nx):
            total = fin[k]
            at = slice(k * cut, (k + 1) * cut)
            gq_ref[:, at] = total[:share, :cut]
            go_ref[:, at] = total[:share, cut:]
            gkv_ref[:, at] = total[share:, :cut]
            gkv_ref[:, width + k * cut : width + (k + 1) * cut] = total[share:, cut:]

    spread(0)
    loaded("mem")
    serve(0, 0, mem_ref)
    serve(0, 1, mem_ref)
    spread(1)
    loaded("nidx", "feat", "wkv", "wo", "cot")
    prepare(0)
    name_rows(0)
    ask_all(1)
    loaded("gi", "gh", "wq")
    fetch(0)
    update(0, 0)
    update(0, 1)
    attend(0)
    attend_back(0)
    embed(0)
    for t in range(2):
        apply(0, t, mem_ref, mem1)
        serve(1, t, mem1)
    prepare(1)
    name_rows(1)
    fetch(1)
    update(1, 0)
    attend(1)
    reduce_core(1)
    attend_back(1)
    reduce_core(0)
    reduce_x(1)
    update(1, 1)
    reduce_x(0)
    embed(1)
    reduce_y(1)
    reduce_y(0)
    apply(1, 0, mem1, newmem_ref)
    reduce_z()
    share_x()
    apply(1, 1, mem1, newmem_ref, store_memory)
    finish()

    for b in range(2):
        for t in range(2):
            wait_sent(others(served, b, t), 1 + 2 * b + t)
            wait_sent(others(outgoing, b, t), 5 + 2 * b + t)
        store_embeddings(b).wait()
    wait_sent(ids_out.at[pl.ds(0, n - 1)], 0)
    for t in range(2):
        wait_sent(r1.at[t], 9 + t)
        if nx > 1:
            wait_sent(r2.at[t], 11 + t)
        wait_sent(r3.at[t], 13 + t)
    if nz > 1:
        wait_sent(r4, 15)
    if nx > 1:
        wait_sent(fin.at[pl.ds(0, nx - 1)], 16)
    for k in range(nodes // step):
        store_memory(k).wait()


def hand_on(*refs):
    count = (len(refs) - 1) // 3
    sem = refs[-1]
    steps = []
    for src, dst, held in zip(refs[:count], refs[count : 2 * count], refs[2 * count : 3 * count]):
        rows = src.shape[0]
        pieces = 8 if rows % 128 == 0 else 1
        for k in range(pieces):
            at = pl.ds(k * (rows // pieces), rows // pieces)
            get = pltpu.make_async_copy(src.at[at], held.at[at], sem.at[0, len(steps)])
            put = pltpu.make_async_copy(held.at[at], dst.at[at], sem.at[1, len(steps)])
            get.start()
            steps.append((get, put))
    for get, put in steps:
        get.wait()
        put.start()
    for _, put in steps:
        put.wait()


def on_device(
    memory,
    endpoint_owner,
    endpoint_row,
    event_time,
    neighbour_time,
    neighbour_feat,
    neighbour_index,
    valid_length,
    decay_rate,
    w_query,
    w_keyval,
    w_out,
    gru_input,
    gru_hidden,
    cotangent,
):
    n = lax.axis_size("mem")
    nx = lax.axis_size("rep")
    nz = n // PLANE
    _, nodes, width = memory.shape
    batches, events = event_time.shape[1:]
    nbrs = neighbour_time.shape[2]
    listed = neighbour_index.shape[3]
    ends = 2 * events
    slots = n * CAP
    part = 2 * width // n
    plane = nz * part
    half = n // 2 * part
    cut = width // nx
    owner = endpoint_owner[0].transpose(0, 2, 1)
    row = endpoint_row[0].transpose(0, 2, 1)
    vmem = pl.BlockSpec(memory_space=pltpu.VMEM)
    shape = jax.ShapeDtypeStruct
    share = width // n
    hbm = pl.BlockSpec(memory_space=pl.ANY)
    outputs = (
        shape((nodes, width), BF),
        shape((batches, events, width), BF),
        shape((share, width), F32),
        shape((share, 2 * width), F32),
        shape((share, width), F32),
    )
    results = pl.pallas_call(
        functools.partial(window, nx),
        out_shape=outputs,
        in_specs=[vmem] * 5 + [pl.BlockSpec(memory_space=pltpu.SMEM)] + [hbm] * 9,
        out_specs=(hbm,) * 2 + (vmem,) * 3,
        scratch_shapes=[
            pltpu.VMEM((batches, events, listed), I32),
            pltpu.VMEM((nodes, width), BF),
            pltpu.VMEM((batches, nbrs, width), BF),
            pltpu.VMEM((batches, events, width), BF),
            pltpu.VMEM((width, width), BF),
            pltpu.VMEM((width, 2 * width), BF),
            pltpu.VMEM((width, width), BF),
            pltpu.VMEM((width, 3 * width), BF),
            pltpu.VMEM((width, 3 * width), BF),
            pltpu.VMEM((nodes, width), BF),
            pltpu.VMEM((batches, events, width), BF),
            pltpu.SemaphoreType.DMA((9,)),
            pltpu.SemaphoreType.DMA((2 + nodes // min(512, nodes),)),
            pltpu.VMEM((n, 1, 256), I32),
            pltpu.VMEM((n, 1, 256), I32),
            pltpu.VMEM((batches, slots, width), BF),
            pltpu.VMEM((batches, slots, width), BF),
            pltpu.VMEM((batches, slots, width), BF),
            pltpu.VMEM((batches, slots, width), BF),
            pltpu.VMEM((nodes, width), BF),
            pltpu.VMEM((8, ends), I32),
            pltpu.VMEM((8, slots), I32),
            pltpu.VMEM((batches, slots, 128), I32),
            pltpu.VMEM((ends, slots), BF),
            pltpu.VMEM((slots, ends), BF),
            pltpu.VMEM((slots, nodes), BF),
            pltpu.VMEM((nodes, slots), BF),
            pltpu.VMEM((nodes, 128), F32),
            pltpu.VMEM((batches, 2, events, width), BF),
            pltpu.VMEM((ends, width), BF),
            pltpu.VMEM((listed, events), I32),
            pltpu.VMEM((nbrs, events), F32),
            pltpu.VMEM((HEADS, nbrs, events), F32),
            pltpu.VMEM((HEADS, nbrs, events), F32),
            pltpu.VMEM((nbrs, 2 * width), BF),
            pltpu.VMEM((2 * width, nbrs), BF),
            pltpu.VMEM((events, width), BF),
            pltpu.VMEM((events, width), BF),
            pltpu.VMEM((width, events), BF),
            pltpu.VMEM((width, events), BF),
            pltpu.VMEM((nbrs, 2 * width), BF),
            pltpu.VMEM((width, 2 * width), F32),
            pltpu.VMEM((width, 2 * width), F32),
            pltpu.VMEM((2, 2, nx, half, cut), BF),
            pltpu.VMEM((2, nx, half, cut), BF),
            pltpu.VMEM((2, nx, half, cut), BF),
            pltpu.VMEM((2, max(nx - 1, 1), half, cut), BF),
            pltpu.VMEM((2, half, cut), BF),
            pltpu.VMEM((2, NY - 1, plane, cut), BF),
            pltpu.VMEM((plane, 2 * cut), BF),
            pltpu.VMEM((max(nz - 1, 1), part, 2 * cut), BF),
            pltpu.VMEM((nx, part, 2 * cut), F32),
            pltpu.SemaphoreType.DMA((17,)),
            pltpu.SemaphoreType.DMA((17,)),
        ],
        compiler_params=pltpu.CompilerParams(
            collective_id=0, has_side_effects=True, vmem_limit_bytes=60 * 1024 * 1024
        ),
        name="window",
    )(
        owner,
        row,
        event_time[0],
        neighbour_time[0],
        valid_length[0],
        decay_rate,
        neighbour_index[0],
        memory[0],
        neighbour_feat[0],
        cotangent[0],
        w_query,
        w_keyval,
        w_out,
        gru_input,
        gru_hidden,
    )
    new_memory, embeddings, gq, gkv, go = pl.pallas_call(
        hand_on,
        out_shape=outputs,
        in_specs=[hbm] * 5,
        out_specs=(hbm,) * 5,
        scratch_shapes=[pltpu.VMEM(out.shape, out.dtype) for out in outputs] + [pltpu.SemaphoreType.DMA((2, 16))],
        compiler_params=pltpu.CompilerParams(vmem_limit_bytes=60 * 1024 * 1024),
        name="hand_on",
    )(*results)
    return (new_memory[None], embeddings[None], gq, gkv, go)


def solution(mesh):
    return jax.shard_map(
        on_device,
        mesh=mesh,
        in_specs=(
            P("rep", "mem", None),
            P("rep", None, "mem", None),
            P("rep", None, "mem", None),
            P("rep", None, "mem"),
            P("rep", None, "mem"),
            P("rep", None, "mem", None),
            P("rep", None, "mem", None),
            P("rep", None, "mem"),
            P(),
            P(),
            P(),
            P(),
            P(),
            P(),
            P("rep", None, "mem", None),
        ),
        out_specs=(
            P("rep", "mem", None),
            P("rep", None, "mem", None),
            P("mem", None),
            P("mem", None),
            P("mem", None),
        ),
        check_vma=False,
    )
```
